32 devices in a mesh: groups: 2 (over x), ctx: 8 (over z, y), head: 2 (over core).
Axes of the slice: x: 2, y: 2, z: 4, core: 2. Of those that a mesh axis runs over, the one named last changes fastest.
Arguments:
- queries: bfloat16 [4096, 4, 8, 128], P(('groups', 'ctx'), 'head'), parts along dimension 0, may hold values from -40 to 40
- keys: bfloat16 [4096, 4, 128], P(('groups', 'ctx'), 'head'), parts along dimension 0, may hold values from -6 to 6
- values: bfloat16 [4096, 4, 128], P(('groups', 'ctx'), 'head'), parts along dimension 0, may hold values from -6 to 6
- segments: int32 [4096], P(('groups', 'ctx')), parts along dimension 0, may hold values from 0 to 3, never falling along the last dimension, each value on 1 to 1024 neighbouring positions
- score_weight: bfloat16 [4, 8, 128], P('head'), may hold values from -0.09375 to 0.09375
Outputs:
- attended: bfloat16 [4096, 4, 8, 128], P(('groups', 'ctx'), 'head'), parts along dimension 0
- score: float32 [4096], P(('groups', 'ctx')), parts along dimension 0
The draws below stay inside these ranges and needn't reach their ends.
There are 2 independent parts, one for each index of `groups`. The reference program is written for one: setup_inputs(seed, part) draws one part's arguments, and reference() takes and returns one part's arrays. A program takes and returns all parts, laid end to end along the dimension named above; an argument that names none is the same for every part. Nothing has to cross between parts.
Inputs may be any that keep to these rules, and one draw needn't show every extreme that they name: `segments`: document ids never fall along the sequence; each document covers 1 to 1024 positions and one covers exactly 1024.
All inputs are finite; a program needn't handle non-finite values.
Results may differ from the reference program's by a relative error of at most 0.0032.
Values may be sent and summed in bfloat16 or wider, within the bound.
No kernel may reach another device: no remote copies, remote signals or barrier semaphores. Data moves between devices by JAX's collectives and lax.ppermute only.
A program may use at most 64 MiB of HBM per device.

```python
import math
import jax
import jax.numpy as jnp
import numpy as np
from jax import lax

KVH = 4
GROUP = 8
HD = 128
DOCS = 4
SEQ = 2048


def draw_pair(key):
    key_vals = jnp.clip(jax.random.normal(jax.random.fold_in(key, 11), (SEQ, KVH, HD), jnp.float32), -6.0, 6.0)
    query_vals = 2.5 * jnp.clip(jax.random.normal(jax.random.fold_in(key, 12), (SEQ, KVH, GROUP, HD), jnp.float32), -6.0, 6.0)
    return (key_vals, query_vals)


def draw_queries(key, part):
    return draw_pair(key)[1].astype(jnp.bfloat16)


def draw_keys(key, part):
    return draw_pair(key)[0].astype(jnp.bfloat16)


def shard_levels(stream_key, dims, split, least, high):
    factor_of, own = 1.0, jax.random.fold_in(stream_key, 6)
    for axis_at, blocks in split:
        heights = jnp.exp(jax.random.uniform(jax.random.fold_in(own, axis_at), (blocks,), jnp.float32, least / len(split), high / len(split)))
        factor_of = factor_of * jnp.repeat(heights, dims[axis_at] // blocks).reshape([-1 if axis == axis_at else 1 for axis in range(len(dims))])
    return factor_of


def split_up(count, total, limit, slope):
    weights = [(1 << 20) // math.isqrt(grade ** slope) + 1 for grade in range(2, count + 1)]
    spare, counts = total - limit - (count - 1), [1] * (count - 1)
    while spare > 0:
        candidates = [i for i in range(count - 1) if counts[i] < limit]
        mass, remaining = sum([weights[i] for i in candidates]), spare
        for i in candidates:
            more = min(limit - counts[i], max(1, remaining * weights[i] // mass), spare)
            counts[i] = counts[i] + more
            spare = spare - more
    return np.array([limit] + counts)


def ragged(key, count, total, reach, slope):
    if count == 2:
        one = jax.random.randint(key, (), max(1, total - reach), min(reach, total - 1) + 1)
        return jnp.stack([one, total - one])
    tallies = jnp.asarray(split_up(count, total, reach, slope), jnp.int32)
    twos = (count - 1) // 2
    source_of, taker = tallies[1:1 + 2 * twos:2], tallies[2:2 + 2 * twos:2]
    margin = jnp.minimum(source_of - 1, reach - taker)
    passed = jax.random.randint(jax.random.fold_in(key, 1), (twos,), 0, 1 << 20) % (margin + 1)
    tallies = tallies.at[1:1 + 2 * twos:2].set(source_of - passed).at[2:2 + 2 * twos:2].set(taker + passed)
    return tallies[jax.random.permutation(jax.random.fold_in(key, 2), count)]


def normal_values(rng, dims, spread, reach, cuts=(), kind=jnp.bfloat16):
    array = spread * jax.random.normal(rng, dims, jnp.float32)
    if cuts:
        array = array * shard_levels(rng, dims, cuts, -0.22, 0.18)
    return jnp.clip(array, -reach, reach).astype(kind)


def setup_inputs(seed: int = 0, part: int = 0) -> dict:
    streams_of = jax.random.split(jax.random.key(seed), 6)
    part_keys = jax.random.split(jax.random.fold_in(streams_of[5], part), 6)
    return {
        "queries": draw_queries(jax.random.fold_in(jax.random.fold_in(streams_of[5], part), 71), part),
        "keys": draw_keys(jax.random.fold_in(jax.random.fold_in(streams_of[5], part), 71), part),
        "values": normal_values(part_keys[2], (SEQ, KVH, HD), 1.0, 6.0, ((0, 8), (1, 2))),
        "segments": jnp.searchsorted(jnp.cumsum(ragged(part_keys[3], DOCS, SEQ, SEQ // 2, 0)), jnp.arange(SEQ), side="right").astype(jnp.int32),
        "score_weight": normal_values(streams_of[4], (KVH, GROUP, HD), (KVH * GROUP * HD) ** -0.5, 0.09375, ((0, 2),)),
    }


def reference(queries, keys, values, segments, score_weight):
    seq_len = queries.shape[0]
    head_dim = queries.shape[-1]
    block_len = math.gcd(seq_len, 1024)
    positions = jnp.arange(seq_len, dtype=jnp.int32)
    pieces = []
    for block_index in range(seq_len // block_len):
        first = block_index * block_len
        last = first + block_len
        query_pos = positions[first:last]
        query_seg = segments[first:last]
        visible = (positions[None, :last] <= query_pos[:, None]) & (segments[None, :last] == query_seg[:, None])
        head_mask = visible[:, None, :]
        head_inputs = (jnp.transpose(queries[first:last], (1, 0, 2, 3)), jnp.transpose(keys[:last], (1, 0, 2)), jnp.transpose(values[:last], (1, 0, 2)))

        def one_head(inputs):
            query_head, key_head, value_head = inputs
            scores = jnp.einsum('qgd,nd->qgn', query_head.astype(jnp.float32), key_head.astype(jnp.float32)) / math.sqrt(head_dim)
            scores = jnp.where(head_mask, scores, -1e+30)
            row_max = lax.optimization_barrier(jnp.max(scores, axis=-1, keepdims=True))
            weights = jnp.where(head_mask, jnp.exp(scores - row_max), 0.0)
            totals = lax.optimization_barrier(jnp.sum(weights, axis=-1, keepdims=True))
            rounded = lax.optimization_barrier(weights.astype(jnp.bfloat16)).astype(jnp.float32)
            summed = jnp.einsum('qgn,nd->qgd', rounded, value_head.astype(jnp.float32))
            return (summed / totals).astype(jnp.bfloat16)
        pieces.append(jnp.transpose(lax.map(one_head, head_inputs), (1, 0, 2, 3)))
    attended = jnp.concatenate(pieces, axis=0)
    score = jnp.einsum('tkgd,kgd->t', attended.astype(jnp.float32), score_weight.astype(jnp.float32))
    return (attended, score)
```

```python
import functools
import math

import jax
import jax.numpy as jnp
from jax import lax
from jax.experimental import pallas as pl
from jax.experimental.pallas import tpu as pltpu
from jax.sharding import PartitionSpec as P

HIDDEN = -1e30
LABEL_ROWS = 16


def pack(keys, values, segments):
    rows = keys.shape[0]
    lanes = math.prod(keys.shape[1:])
    label_lines = -(-rows // lanes)
    labels = (segments + 1).astype(keys.dtype)
    labels = jnp.pad(labels, (0, label_lines * lanes - rows)).reshape(label_lines, lanes)
    labels = jnp.pad(labels, ((0, -label_lines % LABEL_ROWS), (0, 0)))
    return jnp.concatenate([keys.reshape(rows, lanes), values.reshape(rows, lanes), labels], axis=0)


def attend_kernel(sizes, scale, *refs):
    rows, heads, group, dim, tile_pos, count = sizes
    seg_ref, query_ref, weight_ref = refs[:3]
    block_refs = refs[3 : 3 + count]
    out_ref, score_ref, partial_ref = refs[3 + count :]
    per_pos = heads * group
    tile = tile_pos * per_pos
    lanes = heads * dim
    row_head = (lax.broadcasted_iota(jnp.int32, (tile, dim), 0) % per_pos) // group
    key_pos = lax.broadcasted_iota(jnp.int32, (1, rows), 1)
    first_seg = seg_ref[0]
    weight = weight_ref[...].astype(jnp.float32)

    def labels_of(ref):
        lines = -(-rows // lanes)
        grid = ref[2 * rows : 2 * rows + LABEL_ROWS * (-(-lines // LABEL_ROWS)), :].astype(jnp.float32)
        return jnp.concatenate([grid[n : n + 1, :] for n in range(lines)], axis=1)[:, :rows].astype(jnp.int32)

    def step(index, carry):
        start = pl.multiple_of(index * tile, tile)
        query = query_ref[pl.ds(start, tile), :]
        wide = jnp.concatenate(
            [jnp.where(row_head == h, query, jnp.zeros_like(query)) for h in range(heads)], axis=1
        )
        scores = []
        top = None
        for back, ref in enumerate(block_refs):
            labels = labels_of(ref)
            bias = []
            for p in range(tile_pos):
                pos = index * tile_pos + p
                seg = seg_ref[pos]
                if back == 0:
                    seen = (labels == seg + 1) & (key_pos <= pos)
                else:
                    wanted = jnp.where(seg == first_seg, seg + 1, -1)
                    seen = labels == wanted
                bias.append(jnp.broadcast_to(jnp.where(seen, 0.0, HIDDEN), (per_pos, rows)))
            part = lax.dot_general(
                wide, ref[:rows, :], (((1,), (1,)), ((), ())), preferred_element_type=jnp.float32
            )
            part = part + jnp.concatenate(bias, axis=0)
            scores.append(part)
            part_top = jnp.max(part, axis=1, keepdims=True)
            top = part_top if top is None else jnp.maximum(top, part_top)
        total = jnp.zeros((tile, 1), jnp.float32)
        acc = jnp.zeros((tile, lanes), jnp.float32)
        for part, ref in zip(scores, block_refs):
            weights = jnp.exp2((part - top) * scale)
            total = total + jnp.sum(weights, axis=1, keepdims=True)
            acc = acc + jnp.dot(
                weights.astype(jnp.bfloat16), ref[rows : 2 * rows, :], preferred_element_type=jnp.float32
            )
        mine = acc[:, :dim]
        for h in range(1, heads):
            mine = jnp.where(row_head == h, acc[:, h * dim : (h + 1) * dim], mine)
        attended = (mine / total).astype(jnp.bfloat16)
        out_ref[pl.ds(start, tile), :] = attended
        product = attended.astype(jnp.float32).reshape(tile_pos, per_pos, dim) * weight
        partial_ref[pl.ds(pl.multiple_of(index * tile_pos, tile_pos), tile_pos), :] = jnp.sum(product, axis=1)
        return carry

    lax.fori_loop(0, rows // tile_pos, step, 0)
    score_ref[...] = lax.dot_general(
        jnp.ones((8, dim), jnp.float32),
        partial_ref[...],
        (((1,), (1,)), ((), ())),
        preferred_element_type=jnp.float32,
        precision=lax.Precision.HIGHEST,
    )


def local(devices, queries, keys, values, segments, score_weight):
    rows, heads, group, dim = queries.shape
    reach = rows * devices // 2
    back = min(devices - 1, -(-(reach - 1) // rows))

    def shift(array, by):
        return lax.ppermute(array, "ctx", [(i, i + by) for i in range(devices - by)])

    blocks = [pack(keys, values, segments)]
    for distance in range(1, back + 1):
        blocks.append(shift(blocks[max(distance - 2, 0)], min(distance, 2)))

    per_pos = heads * group
    tile_pos = min(16, rows)
    vmem = pl.BlockSpec(memory_space=pltpu.VMEM)
    sizes = (rows, heads, group, dim, tile_pos, len(blocks))
    attended, score = pl.pallas_call(
        functools.partial(attend_kernel, sizes, math.log2(math.e) / math.sqrt(dim)),
        out_shape=(
            jax.ShapeDtypeStruct((rows * per_pos, dim), jnp.bfloat16),
            jax.ShapeDtypeStruct((8, rows), jnp.float32),
        ),
        in_specs=[pl.BlockSpec(memory_space=pltpu.SMEM)] + [vmem] * (2 + len(blocks)),
        out_specs=(vmem, vmem),
        scratch_shapes=[pltpu.VMEM((rows, dim), jnp.float32)],
        compiler_params=pltpu.CompilerParams(vmem_limit_bytes=48 * 1024 * 1024),
    )(segments, queries.reshape(rows * per_pos, dim), score_weight.reshape(per_pos, dim), *blocks)
    score = score[0]
    score = score + lax.ppermute(score, "head", [(0, 1), (1, 0)])
    return attended.reshape(queries.shape), score


def solution(mesh):
    return jax.shard_map(
        functools.partial(local, mesh.shape["ctx"]),
        mesh=mesh,
        in_specs=(
            P(("groups", "ctx"), "head", None, None),
            P(("groups", "ctx"), "head", None),
            P(("groups", "ctx"), "head", None),
            P(("groups", "ctx")),
            P("head", None, None),
        ),
        out_specs=(P(("groups", "ctx"), "head", None, None), P(("groups", "ctx"))),
        check_vma=False,
    )
```

```python
import functools
import math

import jax
import jax.numpy as jnp
from jax import lax
from jax.experimental import pallas as pl
from jax.experimental.pallas import tpu as pltpu
from jax.sharding import PartitionSpec as P

HIDDEN = -1e30
LABEL_ROWS = 16


def pack(keys, values, segments):
    rows = keys.shape[0]
    lanes = math.prod(keys.shape[1:])
    label_lines = -(-rows // lanes)
    labels = (segments + 1).astype(keys.dtype)
    labels = jnp.pad(labels, (0, label_lines * lanes - rows)).reshape(label_lines, lanes)
    labels = jnp.pad(labels, ((0, -label_lines % LABEL_ROWS), (0, 0)))
    return jnp.concatenate([keys.reshape(rows, lanes), values.reshape(rows, lanes), labels], axis=0)


def attend_kernel(sizes, scale, first, last, *refs):
    rows, heads, group, dim, tile_pos, count = sizes
    refs = list(refs)
    seg_ref, query_ref = refs[:2]
    block_refs = refs[2 : 2 + count]
    refs = refs[2 + count :]
    if not first:
        old_top_ref, old_total_ref, old_acc_ref = refs[:3]
        refs = refs[3:]
    if last:
        weight_ref, out_ref, score_ref, partial_ref = refs
    else:
        top_ref, total_ref, acc_ref = refs
    per_pos = heads * group
    tile = tile_pos * per_pos
    half = tile_pos * group
    lanes = heads * dim
    key_pos = lax.broadcasted_iota(jnp.int32, (1, rows), 1)
    first_seg = seg_ref[0]

    def labels_of(ref):
        lines = -(-rows // lanes)
        grid = ref[2 * rows : 2 * rows + LABEL_ROWS * (-(-lines // LABEL_ROWS)), :].astype(jnp.float32)
        return jnp.concatenate([grid[n : n + 1, :] for n in range(lines)], axis=1)[:, :rows].astype(jnp.int32)

    def step(index, carry):
        start = pl.multiple_of(index * tile, tile)
        query = query_ref[pl.ds(start, tile), :].astype(jnp.float32).reshape(tile_pos, heads, group, dim)
        biases = []
        for n, ref in enumerate(block_refs):
            labels = labels_of(ref)
            bias = []
            for p in range(tile_pos):
                pos = index * tile_pos + p
                seg = seg_ref[pos]
                if first and n == 0:
                    seen = (labels == seg + 1) & (key_pos <= pos)
                else:
                    seen = labels == jnp.where(seg == first_seg, seg + 1, -1)
                bias.append(jnp.broadcast_to(jnp.where(seen, 0.0, HIDDEN), (group, rows)))
            biases.append(jnp.concatenate(bias, axis=0))
        if not first:
            old_top, old_total, old_acc = (
                ref[pl.ds(start, tile), :].reshape(tile_pos, heads, group, dim)
                for ref in (old_top_ref, old_total_ref, old_acc_ref)
            )
        tops, totals, accs = [], [], []
        for h in range(heads):
            at = slice(h * dim, (h + 1) * dim)
            query_h = query[:, h].reshape(half, dim).astype(jnp.bfloat16)
            top = None if first else old_top[:, h].reshape(half, dim)[:, :1]
            scores = []
            for ref, bias in zip(block_refs, biases):
                part = lax.dot_general(
                    query_h, ref[:rows, at], (((1,), (1,)), ((), ())), preferred_element_type=jnp.float32
                )
                part = part + bias
                scores.append(part)
                part_top = jnp.max(part, axis=1, keepdims=True)
                top = part_top if top is None else jnp.maximum(top, part_top)
            if first:
                total, acc = None, None
            else:
                factor = jnp.exp2((old_top[:, h].reshape(half, dim) - top) * scale)
                total = (old_total[:, h].reshape(half, dim) * factor)[:, :1]
                acc = old_acc[:, h].reshape(half, dim) * factor
            for part, ref in zip(scores, block_refs):
                weights = jnp.exp2((part - top) * scale)
                part_total = jnp.sum(weights, axis=1, keepdims=True)
                part_acc = jnp.dot(
                    weights.astype(jnp.bfloat16), ref[rows : 2 * rows, at], preferred_element_type=jnp.float32
                )
                total = part_total if total is None else total + part_total
                acc = part_acc if acc is None else acc + part_acc
            shape = (tile_pos, 1, group, dim)
            if last:
                accs.append((acc / total).reshape(shape))
            else:
                tops.append(jnp.broadcast_to(top, acc.shape).reshape(shape))
                totals.append(jnp.broadcast_to(total, acc.shape).reshape(shape))
                accs.append(acc.reshape(shape))

        def whole(parts):
            return jnp.concatenate(parts, axis=1).reshape(tile, dim)

        if last:
            attended = whole(accs).astype(jnp.bfloat16)
            out_ref[pl.ds(start, tile), :] = attended
            weight = weight_ref[...].astype(jnp.float32)
            product = attended.astype(jnp.float32).reshape(tile_pos, per_pos, dim) * weight
            partial_ref[pl.ds(pl.multiple_of(index * tile_pos, tile_pos), tile_pos), :] = jnp.sum(product, axis=1)
        else:
            top_ref[pl.ds(start, tile), :] = whole(tops)
            total_ref[pl.ds(start, tile), :] = whole(totals)
            acc_ref[pl.ds(start, tile), :] = whole(accs)
        return carry

    lax.fori_loop(0, rows // tile_pos, step, 0)
    if last:
        score_ref[...] = lax.dot_general(
            jnp.ones((8, dim), jnp.float32),
            partial_ref[...],
            (((1,), (1,)), ((), ())),
            preferred_element_type=jnp.float32,
            precision=lax.Precision.HIGHEST,
        )


def attend(shape, segments, query, blocks, state, weight):
    rows, heads, group, dim = shape
    per_pos = heads * group
    tile_pos = math.gcd(rows, 64)
    vmem = pl.BlockSpec(memory_space=pltpu.VMEM)
    first, last = state is None, weight is not None
    operands = [segments, query, *blocks, *(state or ()), *((weight,) if last else ())]
    flat = (rows * per_pos, dim)
    if last:
        out_shape = (jax.ShapeDtypeStruct(flat, jnp.bfloat16), jax.ShapeDtypeStruct((8, rows), jnp.float32))
    else:
        out_shape = (jax.ShapeDtypeStruct(flat, jnp.float32),) * 3
    work = 4 * rows * per_pos * dim * rows * len(blocks)
    return pl.pallas_call(
        functools.partial(
            attend_kernel,
            (rows, heads, group, dim, tile_pos, len(blocks)),
            math.log2(math.e) / math.sqrt(dim),
            first,
            last,
        ),
        out_shape=out_shape,
        in_specs=[pl.BlockSpec(memory_space=pltpu.SMEM)] + [vmem] * (len(operands) - 1),
        out_specs=(vmem,) * len(out_shape),
        scratch_shapes=[pltpu.VMEM((rows, dim), jnp.float32)] if last else [],
        cost_estimate=pl.CostEstimate(
            flops=work, bytes_accessed=rows * per_pos * dim * 8, transcendentals=work // (4 * dim)
        ),
        compiler_params=pltpu.CompilerParams(vmem_limit_bytes=32 * 1024 * 1024),
    )(*operands)


def local(devices, queries, keys, values, segments, score_weight):
    rows, heads, group, dim = queries.shape
    reach = rows * devices // 2
    back = min(devices - 1, -(-(reach - 1) // rows))

    def shift(array, by):
        return lax.ppermute(array, "ctx", [(i, i + by) for i in range(devices - by)])

    blocks = [pack(keys, values, segments)]
    for distance in range(1, back + 1):
        blocks.append(shift(blocks[max(distance - 2, 0)], min(distance, 2)))

    query = queries.reshape(rows * heads * group, dim)
    weight = score_weight.reshape(heads * group, dim)
    state = None
    for at in range(-1, back, 2):
        ends = at + 2 >= back
        state = attend(
            queries.shape, segments, query, blocks[max(at, 0) : at + 2], state, weight if ends else None
        )
    attended, score = state
    score = score[0]
    score = score + lax.ppermute(score, "head", [(0, 1), (1, 0)])
    return attended.reshape(queries.shape), score


def solution(mesh):
    return jax.shard_map(
        functools.partial(local, mesh.shape["ctx"]),
        mesh=mesh,
        in_specs=(
            P(("groups", "ctx"), "head", None, None),
            P(("groups", "ctx"), "head", None),
            P(("groups", "ctx"), "head", None),
            P(("groups", "ctx")),
            P("head", None, None),
        ),
        out_specs=(P(("groups", "ctx"), "head", None, None), P(("groups", "ctx"))),
        check_vma=False,
    )
```

```python
import functools
import math

import jax
import jax.numpy as jnp
from jax import lax
from jax.experimental import pallas as pl
from jax.experimental.pallas import tpu as pltpu
from jax.sharding import PartitionSpec as P

HIDDEN = -1e30
LABEL_ROWS = 16
LANES = 128


def vmem():
    return pl.BlockSpec(memory_space=pltpu.VMEM)


def pack_kernel(key_ref, value_ref, seg_ref, out_ref):
    rows, heads, dim = key_ref.shape
    for h in range(heads):
        at = slice(h * dim, (h + 1) * dim)
        out_ref[:rows, at] = key_ref[:, h, :]
        out_ref[rows : 2 * rows, at] = value_ref[:, h, :]
    labels = (seg_ref[...] + 1).astype(jnp.float32).astype(jnp.bfloat16)
    empty = jnp.zeros((out_ref.shape[0] - 2 * rows - labels.shape[0], labels.shape[1]), jnp.bfloat16)
    out_ref[2 * rows :, :] = jnp.concatenate([labels, empty], axis=0)


def pack(keys, values, segments):
    rows, heads, dim = keys.shape
    lanes = heads * dim
    lines = -(-rows // lanes)
    segments = jnp.pad(segments, (0, lines * lanes - rows), constant_values=-1).reshape(lines, lanes)
    return pl.pallas_call(
        pack_kernel,
        out_shape=jax.ShapeDtypeStruct((2 * rows + lines + -lines % LABEL_ROWS, lanes), keys.dtype),
        in_specs=[vmem()] * 3,
        out_specs=vmem(),
        compiler_params=pltpu.CompilerParams(vmem_limit_bytes=4 * 1024 * 1024),
    )(keys, values, segments)


def attend_kernel(sizes, scale, first, last, *refs):
    rows, heads, group, dim, tile_pos, count = sizes
    refs = list(refs)
    query_ref, own_ref = refs[:2]
    block_refs = [own_ref] if first else refs[2 : 2 + count]
    refs = refs[2 if first else 2 + count + 3 :]
    if last:
        weight_ref, refs = refs[0], refs[1:]
    top_ref, total_ref, acc_ref = refs[:3]
    if last:
        out_ref, score_ref, bias_ref, partial_ref = refs[3:]
    else:
        (bias_ref,) = refs[3:]
    per_pos = heads * group
    tile = tile_pos * per_pos
    half = tile_pos * group
    lanes = heads * dim

    def labels_of(ref):
        lines = -(-rows // lanes)
        grid = ref[2 * rows :, :].astype(jnp.float32)
        return jnp.concatenate([grid[n : n + 1, :] for n in range(lines)], axis=1)[:, :rows]

    own = labels_of(own_ref)
    own_column = jnp.transpose(jnp.broadcast_to(own, (LANES, rows)))[:, :1]
    for n, ref in enumerate(block_refs):
        seen = labels_of(ref) == own_column
        if first:
            seen = seen & (
                lax.broadcasted_iota(jnp.int32, (rows, rows), 1) <= lax.broadcasted_iota(jnp.int32, (rows, rows), 0)
            )
        bias_ref[n] = jnp.where(seen, 0.0, HIDDEN)

    def update(index, blocks, width):
        start = pl.multiple_of(index * tile, tile)
        query = query_ref[pl.ds(start, tile), :].astype(jnp.float32).reshape(tile_pos, heads, group, dim)
        biases = []
        for n in range(len(blocks)):
            lines = [bias_ref[n, pl.ds(index * tile_pos + p, 1), :width] for p in range(tile_pos)]
            biases.append(jnp.concatenate([jnp.broadcast_to(line, (group, width)) for line in lines], axis=0))
        if not first:
            old_top, old_total, old_acc = (
                ref[pl.ds(start, tile), :].reshape(tile_pos, heads, group, dim) for ref in (top_ref, total_ref, acc_ref)
            )
        tops, totals, accs = [], [], []
        for h in range(heads):
            at = slice(h * dim, (h + 1) * dim)
            query_h = query[:, h].reshape(half, dim).astype(jnp.bfloat16)
            scores = []
            for ref, bias in zip(blocks, biases):
                part = lax.dot_general(
                    query_h, ref[:width, at], (((1,), (1,)), ((), ())), preferred_element_type=jnp.float32
                )
                part = part + bias
                scores.extend(part[:, c : c + LANES] for c in range(0, width, LANES))
            old = [] if first else [old_top[:, h].reshape(half, dim)]
            top = jnp.max(functools.reduce(jnp.maximum, old + scores), axis=1, keepdims=True)
            weights = [jnp.exp2((part - top) * scale) for part in scores]
            total = functools.reduce(jnp.add, weights)
            per_block = width // LANES
            acc = None
            for n, ref in enumerate(blocks):
                chunk = jnp.concatenate(
                    [w.astype(jnp.bfloat16) for w in weights[n * per_block : (n + 1) * per_block]], axis=1
                )
                part = jnp.dot(chunk, ref[rows : rows + width, at], preferred_element_type=jnp.float32)
                acc = part if acc is None else acc + part
            if not first:
                factor = jnp.exp2((old[0] - top) * scale)
                total = total + old_total[:, h].reshape(half, dim) * factor
                acc = acc + old_acc[:, h].reshape(half, dim) * factor
            shape = (tile_pos, 1, group, dim)
            tops.append(jnp.broadcast_to(top, acc.shape).reshape(shape))
            totals.append(total.reshape(shape))
            accs.append(acc.reshape(shape))
        for ref, parts in ((top_ref, tops), (total_ref, totals), (acc_ref, accs)):
            ref[pl.ds(start, tile), :] = jnp.concatenate(parts, axis=1).reshape(tile, dim)

    def finish(index):
        start = pl.multiple_of(index * tile, tile)
        total = jnp.sum(total_ref[pl.ds(start, tile), :], axis=1, keepdims=True)
        attended = (acc_ref[pl.ds(start, tile), :] / total).astype(jnp.bfloat16)
        out_ref[pl.ds(start, tile), :] = attended
        weight = weight_ref[...].astype(jnp.float32)
        product = attended.astype(jnp.float32).reshape(tile_pos, per_pos, dim) * weight
        partial_ref[pl.ds(pl.multiple_of(index * tile_pos, tile_pos), tile_pos), :] = jnp.sum(product, axis=1)

    tiles = rows // tile_pos
    if first:
        for index in range(tiles):
            update(index, block_refs, min(rows, -(-((index + 1) * tile_pos) // LANES) * LANES))
    else:
        first_label = jnp.min(own)
        reached = jnp.sum(jnp.where(own == first_label, 1.0, 0.0)).astype(jnp.int32)
        seen_blocks = sum(jnp.where(jnp.max(labels_of(ref)) == first_label, 1, 0) for ref in block_refs)

        def step(index, carry):
            for use in range(1, count + 1):

                @pl.when((seen_blocks == use) & (index * tile_pos < reached))
                def _():
                    update(index, block_refs[:use], rows)

            if last:
                finish(index)
            return carry

        lax.fori_loop(0, tiles, step, 0)
    if last:
        score_ref[...] = lax.dot_general(
            jnp.ones((8, dim), jnp.float32),
            partial_ref[...],
            (((1,), (1,)), ((), ())),
            preferred_element_type=jnp.float32,
            precision=lax.Precision.HIGHEST,
        )


def attend(shape, query, own, blocks, state, weight):
    rows, heads, group, dim = shape
    per_pos = heads * group
    tile_pos = math.gcd(rows, 64)
    first, last = state is None, weight is not None
    operands = [query, own, *blocks, *(state or ()), *((weight,) if last else ())]
    flat = (rows * per_pos, dim)
    out_shape = [jax.ShapeDtypeStruct(flat, jnp.float32)] * 3
    scratch = [pltpu.VMEM((max(len(blocks), 1), rows, rows), jnp.float32)]
    if last:
        out_shape += [jax.ShapeDtypeStruct(flat, jnp.bfloat16), jax.ShapeDtypeStruct((8, rows), jnp.float32)]
        scratch.append(pltpu.VMEM((rows, dim), jnp.float32))
    work = 4 * rows * per_pos * dim * rows * max(len(blocks), 1)
    outs = pl.pallas_call(
        functools.partial(
            attend_kernel,
            (rows, heads, group, dim, tile_pos, len(blocks)),
            math.log2(math.e) / math.sqrt(dim),
            first,
            last,
        ),
        out_shape=out_shape,
        in_specs=[vmem()] * len(operands),
        out_specs=[vmem()] * len(out_shape),
        scratch_shapes=scratch,
        input_output_aliases={} if first else {2 + len(blocks) + n: n for n in range(3)},
        cost_estimate=pl.CostEstimate(
            flops=work, bytes_accessed=rows * per_pos * dim * 8, transcendentals=work // (4 * dim)
        ),
        compiler_params=pltpu.CompilerParams(vmem_limit_bytes=32 * 1024 * 1024),
    )(*operands)
    return outs[3:] if last else outs


def local(devices, queries, keys, values, segments, score_weight):
    rows, heads, group, dim = queries.shape
    reach = rows * devices // 2
    back = min(devices - 1, -(-(reach - 1) // rows))

    def shift(array, by):
        return lax.ppermute(array, "ctx", [(i, i + by) for i in range(devices - by)])

    query = queries.reshape(rows * heads * group, dim)
    weight = score_weight.reshape(heads * group, dim)
    own = pack(keys, values, segments)
    near, far = shift(own, 1), shift(own, 2)
    state = attend(queries.shape, query, own, [], None, None)
    for at in range(1, back + 1, 2):
        near, far, *state = lax.optimization_barrier((near, far, *state))
        blocks = [near, far][: back + 1 - at]
        if at + 2 <= back:
            near, far = shift(near, 2), shift(far, 2)
        state = attend(queries.shape, query, own, blocks, state, weight if at + 2 > back else None)
    attended, score = state
    score = score[0]
    score = score + lax.ppermute(score, "head", [(0, 1), (1, 0)])
    return attended.reshape(queries.shape), score


def solution(mesh):
    return jax.shard_map(
        functools.partial(local, mesh.shape["ctx"]),
        mesh=mesh,
        in_specs=(
            P(("groups", "ctx"), "head", None, None),
            P(("groups", "ctx"), "head", None),
            P(("groups", "ctx"), "head", None),
            P(("groups", "ctx")),
            P("head", None, None),
        ),
        out_specs=(P(("groups", "ctx"), "head", None, None), P(("groups", "ctx"))),
        check_vma=False,
    )
```

```python
import functools
import math

import jax
import jax.numpy as jnp
from jax import lax
from jax.experimental import pallas as pl
from jax.experimental.pallas import tpu as pltpu
from jax.sharding import PartitionSpec as P

HIDDEN = -1e30
LABEL_ROWS = 16
LANES = 128
VMEM = pl.BlockSpec(memory_space=pltpu.VMEM)
HBM = pl.BlockSpec(memory_space=pltpu.HBM)


def whole_permutation(pairs, groups, devices):
    onward = dict(pairs)
    targets = set(onward.values())
    ends = {}
    for start in onward.keys() - targets:
        end = start
        while end in onward:
            end = onward[end]
        ends[end] = start
    idle = [i for i in range(devices) if i not in onward and i not in targets] if groups > 1 else []
    return [
        (g * devices + s, g * devices + t) for g in range(groups) for s, t in sorted({**onward, **ends}.items())
    ] + [(g * devices + i, (g + 1) % groups * devices + i) for g in range(groups) for i in idle]


def pack_kernel(key_hbm, value_hbm, seg_hbm, out_ref, key_ref, value_ref, seg_ref, sems):
    copies = [
        pltpu.make_async_copy(source, target, sems.at[n])
        for n, (source, target) in enumerate(((key_hbm, key_ref), (value_hbm, value_ref), (seg_hbm, seg_ref)))
    ]
    for copy in copies:
        copy.start()
    rows, heads, dim = key_ref.shape
    for n, ref in enumerate((key_ref, value_ref)):
        copies[n].wait()
        for h in range(heads):
            out_ref[n * rows : (n + 1) * rows, h * dim : (h + 1) * dim] = ref[:, h, :]
    copies[2].wait()
    labels = (seg_ref[...] + 1).astype(jnp.float32).astype(jnp.bfloat16)
    empty = jnp.zeros((out_ref.shape[0] - 2 * rows - labels.shape[0], labels.shape[1]), jnp.bfloat16)
    out_ref[2 * rows :, :] = jnp.concatenate([labels, empty], axis=0)


def pack(keys, values, segments):
    rows, heads, dim = keys.shape
    lanes = heads * dim
    lines = -(-rows // lanes)
    segments = jnp.pad(segments, (0, lines * lanes - rows), constant_values=-1).reshape(lines, lanes)
    return pl.pallas_call(
        pack_kernel,
        out_shape=jax.ShapeDtypeStruct((2 * rows + lines + -lines % LABEL_ROWS, lanes), keys.dtype),
        in_specs=[HBM] * 3,
        out_specs=VMEM,
        scratch_shapes=[
            pltpu.VMEM(keys.shape, keys.dtype),
            pltpu.VMEM(values.shape, values.dtype),
            pltpu.VMEM(segments.shape, segments.dtype),
            pltpu.SemaphoreType.DMA((3,)),
        ],
        compiler_params=pltpu.CompilerParams(vmem_limit_bytes=4 * 1024 * 1024),
    )(*(pltpu.with_memory_space_constraint(x, pltpu.HBM) for x in (keys, values, segments)))


def labels_of(ref, rows):
    lines = -(-rows // ref.shape[1])
    grid = ref[2 * rows :, :].astype(jnp.float32)
    return jnp.concatenate([grid[n : n + 1, :] for n in range(lines)], axis=1)[:, :rows]


def fill_bias(bias_ref, labels, own, causal):
    rows = bias_ref.shape[0]
    own_column = jnp.transpose(jnp.broadcast_to(own, (LANES, rows)))[:, :1]
    seen = labels == own_column
    if causal:
        key = lax.broadcasted_iota(jnp.int32, (rows, rows), 1)
        seen = seen & (key <= lax.broadcasted_iota(jnp.int32, (rows, rows), 0))
    bias_ref[...] = jnp.where(seen, 0.0, HIDDEN)


def update(sizes, index, fresh, query_ref, blocks, state_refs):
    rows, heads, group, dim, tile_pos = sizes
    scale = math.log2(math.e) / math.sqrt(dim)
    tile, half = tile_pos * heads * group, tile_pos * group
    start = pl.multiple_of(index * tile, tile)
    query = query_ref[pl.ds(start, tile), :].astype(jnp.float32).reshape(tile_pos, heads, group, dim)
    biases = []
    for _, bias_ref, low, high in blocks:
        lines = [bias_ref[pl.ds(index * tile_pos + p, 1), :][:, low:high] for p in range(tile_pos)]
        biases.append(jnp.concatenate([jnp.broadcast_to(line, (group, high - low)) for line in lines], axis=0))
    if not fresh:
        old_top, old_total, old_acc = (
            ref[pl.ds(start, tile), :].reshape(tile_pos, heads, group, dim) for ref in state_refs
        )
    outs = [], [], []
    for h in range(heads):
        at = slice(h * dim, (h + 1) * dim)
        query_h = query[:, h].reshape(half, dim).astype(jnp.bfloat16)
        scores = []
        for (block_ref, _, low, high), bias in zip(blocks, biases):
            score = lax.dot_general(
                query_h, block_ref[low:high, at], (((1,), (1,)), ((), ())), preferred_element_type=jnp.float32
            )
            score = score + bias
            scores.append([score[:, c : c + LANES] for c in range(0, high - low, LANES)])
        old = [] if fresh else [old_top[:, h].reshape(half, dim)]
        top = jnp.max(functools.reduce(jnp.maximum, sum(scores, old)), axis=1, keepdims=True)
        weights = [[jnp.exp2((part - top) * scale) for part in parts] for parts in scores]
        total = functools.reduce(jnp.add, sum(weights, []))
        acc = None
        for (block_ref, _, low, high), parts in zip(blocks, weights):
            rounded = jnp.concatenate([part.astype(jnp.bfloat16) for part in parts], axis=1)
            part = jnp.dot(rounded, block_ref[rows + low : rows + high, at], preferred_element_type=jnp.float32)
            acc = part if acc is None else acc + part
        if not fresh:
            factor = jnp.exp2((old[0] - top) * scale)
            total = total + old_total[:, h].reshape(half, dim) * factor
            acc = acc + old_acc[:, h].reshape(half, dim) * factor
        for out, part in zip(outs, (jnp.broadcast_to(top, acc.shape), total, acc)):
            out.append(part.reshape(tile_pos, 1, group, dim))
    for ref, parts in zip(state_refs, outs):
        ref[pl.ds(start, tile), :] = jnp.concatenate(parts, axis=1).reshape(tile, dim)


def own_kernel(sizes, query_hbm, block_ref, query_ref, top_ref, total_ref, acc_ref, bias_ref, sems):
    rows, heads, group, _, tile_pos = sizes
    tile = tile_pos * heads * group
    copies = [
        pltpu.make_async_copy(
            query_hbm.at[pl.ds(n * tile, tile), :], query_ref.at[pl.ds(n * tile, tile), :], sems.at[n]
        )
        for n in range(rows // tile_pos)
    ]
    for copy in copies:
        copy.start()
    own = labels_of(block_ref, rows)
    fill_bias(bias_ref, own, own, True)
    for n, copy in enumerate(copies):
        copy.wait()
        high = min(rows, -(-((n + 1) * tile_pos) // LANES) * LANES)
        update(sizes, n, True, query_ref, [(block_ref, bias_ref, 0, high)], (top_ref, total_ref, acc_ref))


def block_kernel(sizes, distances, choices, last, *refs):
    rows, heads, group, dim, tile_pos = sizes
    query_ref, own_ref = refs[:2]
    refs = list(refs[2:])
    choice_refs = [[refs.pop(0) for _ in range(n)] for n in choices]
    del refs[:3]
    weight_ref = refs.pop(0) if last else None
    state_refs, refs = refs[:3], refs[3:]
    if last:
        out_hbm, score_ref, out_ref, partial_ref, sems = refs[:5]
        refs = refs[5:]
    per_pos = heads * group
    tile = tile_pos * per_pos
    tiles = rows // tile_pos
    place = lax.axis_index("ctx")
    bias_refs, refs = refs[: len(choices)], refs[len(choices) :]
    block_refs = []
    for either in choice_refs:
        block_refs.append(either[0] if len(either) == 1 else refs.pop(0))
        if len(either) > 1:
            for parity, ref in enumerate(either):

                @pl.when(place % 2 == parity)
                def _(ref=ref, block_ref=block_refs[-1]):
                    block_ref[...] = ref[...]

    own = labels_of(own_ref, rows)
    first_label = jnp.min(own)
    reached = jnp.sum(jnp.where(own == first_label, 1.0, 0.0)).astype(jnp.int32)
    tiles_reached = (reached + tile_pos - 1) // tile_pos
    labels = [labels_of(ref, rows) for ref in block_refs]
    seen = [(jnp.max(label) == first_label) & (place >= far) for label, far in zip(labels, distances)]
    for n, see in enumerate(seen):

        @pl.when(see)
        def _(n=n):
            fill_bias(bias_refs[n], labels[n], own, False)

    def add(index, count, low=0):
        blocks = [(block_refs[n], bias_refs[n], low, rows) for n in range(count)]
        update(sizes, index, False, query_ref, blocks, state_refs)

    def finish(index):
        start = pl.multiple_of(index * tile, tile)
        total = jnp.sum(state_refs[1][pl.ds(start, tile), :], axis=1, keepdims=True)
        attended = (state_refs[2][pl.ds(start, tile), :] / total).astype(jnp.bfloat16)
        out_ref[pl.ds(start, tile), :] = attended
        pltpu.make_async_copy(
            out_ref.at[pl.ds(start, tile), :], out_hbm.at[pl.ds(start, tile), :], sems.at[index]
        ).start()
        weight = weight_ref[...].astype(jnp.float32)
        product = attended.astype(jnp.float32).reshape(tile_pos, per_pos, dim) * weight
        partial_ref[pl.ds(pl.multiple_of(index * tile_pos, tile_pos), tile_pos), :] = jnp.sum(product, axis=1)

    if last:
        middle = rows // 2 // LANES * LANES
        upper = jnp.max(labels[0][:, :middle]) < first_label if middle else jnp.bool_(False)

        def step(index, carry):
            mine = seen[0] & (index < tiles_reached)

            @pl.when(mine & upper)
            def _():
                add(index, 1, middle)

            @pl.when(mine & jnp.logical_not(upper))
            def _():
                add(index, 1)

            finish(index)
            return carry

        lax.fori_loop(0, tiles, step, 0)
        score_ref[...] = lax.dot_general(
            jnp.ones((8, dim), jnp.float32),
            partial_ref[...],
            (((1,), (1,)), ((), ())),
            preferred_element_type=jnp.float32,
            precision=lax.Precision.HIGHEST,
        )
        for n in range(tiles):
            pltpu.make_async_copy(
                out_ref.at[pl.ds(n * tile, tile), :], out_hbm.at[pl.ds(n * tile, tile), :], sems.at[n]
            ).wait()
    else:
        count = sum(jnp.where(see, 1, 0) for see in seen)
        every = tiles_reached == tiles
        for use in range(1, len(seen) + 1):

            @pl.when((count == use) & every)
            def _(use=use):
                for index in range(tiles):
                    add(index, use)

            @pl.when((count == use) & jnp.logical_not(every))
            def _(use=use):
                def step(index, carry):
                    add(index, use)
                    return carry

                lax.fori_loop(0, tiles_reached, step, 0)


def call(kernel, sizes, blocks, in_specs, out_specs, out_shape, scratch, aliases, operands):
    rows, heads, group, dim, _ = sizes
    work = 4 * rows * heads * group * dim * rows * blocks
    return pl.pallas_call(
        kernel,
        out_shape=out_shape,
        in_specs=in_specs,
        out_specs=out_specs,
        scratch_shapes=scratch,
        input_output_aliases=aliases,
        cost_estimate=pl.CostEstimate(
            flops=work, bytes_accessed=rows * heads * group * dim * 8, transcendentals=work // (4 * dim)
        ),
        compiler_params=pltpu.CompilerParams(vmem_limit_bytes=32 * 1024 * 1024),
    )(*operands)


def attend_own(sizes, query, own):
    rows, heads, group, dim, tile_pos = sizes
    flat = (rows * heads * group, dim)
    return call(
        functools.partial(own_kernel, sizes),
        sizes,
        1,
        [HBM, VMEM],
        [VMEM] * 4,
        [jax.ShapeDtypeStruct(flat, jnp.bfloat16)] + [jax.ShapeDtypeStruct(flat, jnp.float32)] * 3,
        [pltpu.VMEM((rows, rows), jnp.float32), pltpu.SemaphoreType.DMA((rows // tile_pos,))],
        {},
        (pltpu.with_memory_space_constraint(query, pltpu.HBM), own),
    )


def attend_blocks(sizes, distances, query, own, choices, state, weight):
    rows, heads, group, dim, tile_pos = sizes
    flat = (rows * heads * group, dim)
    last = weight is not None
    counts = [len(either) for either in choices]
    operands = [query, own, *sum(choices, []), *state, *((weight,) if last else ())]
    out_shape = [jax.ShapeDtypeStruct(flat, jnp.float32)] * 3
    out_specs = [VMEM] * 3
    scratch = []
    if last:
        out_shape += [jax.ShapeDtypeStruct(flat, jnp.bfloat16), jax.ShapeDtypeStruct((8, rows), jnp.float32)]
        out_specs += [HBM, VMEM]
        scratch += [
            pltpu.VMEM(flat, jnp.bfloat16),
            pltpu.VMEM((rows, dim), jnp.float32),
            pltpu.SemaphoreType.DMA((rows // tile_pos,)),
        ]
    scratch += [pltpu.VMEM((rows, rows), jnp.float32)] * len(choices)
    scratch += [pltpu.VMEM(own.shape, own.dtype) for n in counts if n > 1]
    outs = call(
        functools.partial(block_kernel, sizes, distances, counts, last),
        sizes,
        len(choices),
        [VMEM] * len(operands),
        out_specs,
        out_shape,
        scratch,
        {2 + sum(counts) + n: n for n in range(3)},
        operands,
    )
    return outs[3:] if last else outs


def local(groups, devices, queries, keys, values, segments, score_weight):
    rows, heads, group, dim = queries.shape
    reach = rows * devices // 2
    back = min(devices - 1, -(-(reach - 1) // rows))
    sizes = (rows, heads, group, dim, math.gcd(rows, 64))

    def send(array, pairs):
        return lax.ppermute(array, "ctx", [(s, t) for s, t in pairs if t < devices])

    def send_round(array, by):
        return send(array, [(i, (i + by) % devices) for i in range(devices)])

    def send_even(array, distance):
        pairs = [(i, i + 2) for i in range(distance, devices - 2) if i % 2 == 0]
        return lax.ppermute(array, ("groups", "ctx"), whole_permutation(pairs, groups, devices))

    def send_across(array):
        return send(array, [(i, i ^ 1) for i in range(devices)])

    weight = score_weight.reshape(heads * group, dim)
    own = pack(keys, values, segments)
    far = send_round(own, 2)
    near = [send(own, [(i, i + 1) for i in range(devices)])]
    query, *state = attend_own(sizes, queries.reshape(rows * heads * group, dim), own)
    far, query = lax.optimization_barrier((far, query))
    for distance in range(1, back + 1, 2):
        step = [near, [far]][: back + 1 - distance]
        if distance + 3 <= back:
            next_far = send_round(far, 2)
        if distance + 2 <= back:
            next_near = [send_even(near[0], distance + 1), send_across(far)]
            state = attend_blocks(sizes, (distance, distance + 1), query, own, step, state, None)
            near, far = next_near, next_far if distance + 3 <= back else None
    if len(step) > 1:
        state = attend_blocks(sizes, (distance + 1,), query, own, step[1:], state, None)
    attended, score = attend_blocks(sizes, (distance,), query, own, step[:1], state, weight)
    score = score[0]
    score = score + lax.ppermute(score, "head", [(0, 1), (1, 0)])
    return attended.reshape(queries.shape), score


def solution(mesh):
    return jax.shard_map(
        functools.partial(local, mesh.shape["groups"], mesh.shape["ctx"]),
        mesh=mesh,
        in_specs=(
            P(("groups", "ctx"), "head", None, None),
            P(("groups", "ctx"), "head", None),
            P(("groups", "ctx"), "head", None),
            P(("groups", "ctx")),
            P("head", None, None),
        ),
        out_specs=(P(("groups", "ctx"), "head", None, None), P(("groups", "ctx"))),
        check_vma=False,
    )
```

```python
import functools
import math

import jax
import jax.numpy as jnp
from jax import lax
from jax.experimental import pallas as pl
from jax.experimental.pallas import tpu as pltpu
from jax.sharding import PartitionSpec as P

HIDDEN = -1e30
LABEL_ROWS = 16
LANES = 128
VMEM = pl.BlockSpec(memory_space=pltpu.VMEM)
HBM = pl.BlockSpec(memory_space=pltpu.HBM)


def whole_permutation(pairs, groups, devices):
    onward = dict(pairs)
    targets = set(onward.values())
    ends = {}
    for start in onward.keys() - targets:
        end = start
        while end in onward:
            end = onward[end]
        ends[end] = start
    idle = [i for i in range(devices) if i not in onward and i not in targets] if groups > 1 else []
    return [
        (g * devices + s, g * devices + t) for g in range(groups) for s, t in sorted({**onward, **ends}.items())
    ] + [(g * devices + i, (g + 1) % groups * devices + i) for g in range(groups) for i in idle]


def pack_kernel(key_hbm, value_hbm, seg_hbm, out_ref, key_ref, value_ref, seg_ref, sems):
    copies = [
        pltpu.make_async_copy(source, target, sems.at[n])
        for n, (source, target) in enumerate(((key_hbm, key_ref), (value_hbm, value_ref), (seg_hbm, seg_ref)))
    ]
    for copy in copies:
        copy.start()
    rows, heads, dim = key_ref.shape
    for n, ref in enumerate((key_ref, value_ref)):
        copies[n].wait()
        for h in range(heads):
            out_ref[n * rows : (n + 1) * rows, h * dim : (h + 1) * dim] = ref[:, h, :]
    copies[2].wait()
    labels = (seg_ref[...] + 1).astype(jnp.float32).astype(jnp.bfloat16)
    empty = jnp.zeros((out_ref.shape[0] - 2 * rows - labels.shape[0], labels.shape[1]), jnp.bfloat16)
    out_ref[2 * rows :, :] = jnp.concatenate([labels, empty], axis=0)


def pack(keys, values, segments):
    rows, heads, dim = keys.shape
    lanes = heads * dim
    lines = -(-rows // lanes)
    segments = jnp.pad(segments, (0, lines * lanes - rows), constant_values=-1).reshape(lines, lanes)
    return pl.pallas_call(
        pack_kernel,
        out_shape=jax.ShapeDtypeStruct((2 * rows + lines + -lines % LABEL_ROWS, lanes), keys.dtype),
        in_specs=[HBM] * 3,
        out_specs=VMEM,
        scratch_shapes=[
            pltpu.VMEM(keys.shape, keys.dtype),
            pltpu.VMEM(values.shape, values.dtype),
            pltpu.VMEM(segments.shape, segments.dtype),
            pltpu.SemaphoreType.DMA((3,)),
        ],
        compiler_params=pltpu.CompilerParams(vmem_limit_bytes=4 * 1024 * 1024),
    )(*(pltpu.with_memory_space_constraint(x, pltpu.HBM) for x in (keys, values, segments)))


def labels_of(ref, rows):
    lines = -(-rows // ref.shape[1])
    grid = ref[2 * rows :, :].astype(jnp.float32)
    return jnp.concatenate([grid[n : n + 1, :] for n in range(lines)], axis=1)[:, :rows]


def fill_bias(bias_ref, labels, own, causal):
    rows = bias_ref.shape[0]
    own_column = jnp.transpose(jnp.broadcast_to(own, (LANES, rows)))[:, :1]
    seen = labels == own_column
    if causal:
        key = lax.broadcasted_iota(jnp.int32, (rows, rows), 1)
        seen = seen & (key <= lax.broadcasted_iota(jnp.int32, (rows, rows), 0))
    bias_ref[...] = jnp.where(seen, 0.0, HIDDEN)


def update(sizes, tile_pos, index, fresh, query_ref, blocks, state_refs):
    rows, heads, group, dim = sizes
    scale = math.log2(math.e) / math.sqrt(dim)
    tile, half = tile_pos * heads * group, tile_pos * group
    start = pl.multiple_of(index * tile, tile)
    query = query_ref[pl.ds(start, tile), :].astype(jnp.float32).reshape(tile_pos, heads, group, dim)
    biases = []
    for _, bias, low, high in blocks:
        if bias is None:
            biases.append(None)
        elif isinstance(bias, jax.Array):
            biases.append(jnp.broadcast_to(bias[:, low:high], (half, high - low)))
        else:
            lines = [bias[pl.ds(index * tile_pos + p, 1), :][:, low:high] for p in range(tile_pos)]
            biases.append(jnp.concatenate([jnp.broadcast_to(line, (group, high - low)) for line in lines], axis=0))
    if not fresh:
        old_top, old_total, old_acc = (
            ref[pl.ds(start, tile), :].reshape(tile_pos, heads, group, dim) for ref in state_refs
        )
    outs = [], [], []
    for h in range(heads):
        at = slice(h * dim, (h + 1) * dim)
        query_h = query[:, h].reshape(half, dim).astype(jnp.bfloat16)
        scores = []
        for (block_ref, _, low, high), bias in zip(blocks, biases):
            score = lax.dot_general(
                query_h, block_ref[low:high, at], (((1,), (1,)), ((), ())), preferred_element_type=jnp.float32
            )
            if bias is not None:
                score = score + bias
            scores.append([score[:, c : c + LANES] for c in range(0, high - low, LANES)])
        old = [] if fresh else [old_top[:, h].reshape(half, dim)]
        top = jnp.max(functools.reduce(jnp.maximum, sum(scores, old)), axis=1, keepdims=True)
        weights = [[jnp.exp2((part - top) * scale) for part in parts] for parts in scores]
        total = functools.reduce(jnp.add, sum(weights, []))
        acc = None
        for (block_ref, _, low, high), parts in zip(blocks, weights):
            rounded = jnp.concatenate([part.astype(jnp.bfloat16) for part in parts], axis=1)
            part = jnp.dot(rounded, block_ref[rows + low : rows + high, at], preferred_element_type=jnp.float32)
            acc = part if acc is None else acc + part
        if not fresh:
            factor = jnp.exp2((old[0] - top) * scale)
            total = total + old_total[:, h].reshape(half, dim) * factor
            acc = acc + old_acc[:, h].reshape(half, dim) * factor
        for out, part in zip(outs, (jnp.broadcast_to(top, acc.shape), total, acc)):
            out.append(part.reshape(tile_pos, 1, group, dim))
    for ref, parts in zip(state_refs, outs):
        ref[pl.ds(start, tile), :] = jnp.concatenate(parts, axis=1).reshape(tile, dim)


def own_kernel(sizes, tile_pos, query_hbm, block_ref, query_ref, top_ref, total_ref, acc_ref, bias_ref, sems):
    rows, heads, group, _ = sizes
    tile = tile_pos * heads * group
    copies = [
        pltpu.make_async_copy(
            query_hbm.at[pl.ds(n * tile, tile), :], query_ref.at[pl.ds(n * tile, tile), :], sems.at[n]
        )
        for n in range(rows // tile_pos)
    ]
    for copy in copies:
        copy.start()
    own = labels_of(block_ref, rows)
    fill_bias(bias_ref, own, own, True)
    for n, copy in enumerate(copies):
        copy.wait()
        high = min(rows, -(-((n + 1) * tile_pos) // LANES) * LANES)
        update(sizes, tile_pos, n, True, query_ref, [(block_ref, bias_ref, 0, high)], (top_ref, total_ref, acc_ref))


class Blocks:
    def __init__(self, sizes, distances, counts, picks, refs, always=False):
        self.sizes, (rows, heads, group, dim) = sizes, sizes
        refs = list(refs)
        self.query_ref, own_ref = refs.pop(0), refs.pop(0)
        either_refs = [[refs.pop(0) for _ in range(n)] for n in counts]
        del refs[:3]
        self.rest = refs
        bias_and_copies = refs.pop()
        self.bias_refs = bias_and_copies[: len(counts)]
        copies = list(bias_and_copies[len(counts) :])
        place = lax.axis_index("ctx")
        self.block_refs = []
        for either, pick in zip(either_refs, picks):
            self.block_refs.append(either[0] if len(either) == 1 else copies.pop(0))
            if len(either) > 1:
                for n, ref in enumerate(either):

                    @pl.when(pick(place) == n)
                    def _(ref=ref, block_ref=self.block_refs[-1]):
                        block_ref[...] = ref[...]

        own = labels_of(own_ref, rows)
        first_label = jnp.min(own)
        self.reached = jnp.sum(jnp.where(own == first_label, 1.0, 0.0)).astype(jnp.int32)
        labels = [labels_of(ref, rows) for ref in self.block_refs]
        self.seen = [(jnp.max(label) == first_label) & (place >= far) for label, far in zip(labels, distances)]
        self.full = [see & (jnp.min(label) == first_label) for label, see in zip(labels, self.seen)]
        self.middle = rows // 2 // LANES * LANES
        self.upper = [
            jnp.max(label[:, : self.middle]) < first_label if self.middle else jnp.bool_(False) for label in labels
        ]
        self.key_bias = [jnp.where(label == first_label, 0.0, HIDDEN) for label in labels]
        for n, see in enumerate(self.seen):

            @pl.when(see & (always | (self.reached < rows)))
            def _(n=n):
                fill_bias(self.bias_refs[n], labels[n], own, False)

    def add(self, state_refs, tile_pos, index, biases, low=0):
        blocks = [(self.block_refs[n], bias, low, self.sizes[0]) for n, bias in enumerate(biases)]
        update(self.sizes, tile_pos, index, False, self.query_ref, blocks, state_refs)

    def add_all(self, state_refs, large, small):
        many = len(self.seen)
        whole = self.reached // large
        end = (self.reached + small - 1) // small
        zero = jnp.int32(0)
        for count in range(1, many + 1):
            wanted = self.seen[count - 1]
            if count < many:
                wanted = wanted & jnp.logical_not(self.seen[count])
            nearer, rows_bias = [None] * (count - 1), self.key_bias[count - 1]
            full, upper = self.full[count - 1], self.upper[count - 1]
            cases = [(wanted & jnp.logical_not(full | upper), rows_bias, 0)]
            if count == many:
                cases.append((wanted & full, None, 0))
            else:
                cases[0] = (wanted & jnp.logical_not(upper), rows_bias, 0)
            if many == 1 and self.middle:
                cases.append((wanted & upper, rows_bias, self.middle))
            else:
                cases[0] = (cases[0][0] | (wanted & upper), rows_bias, 0)
            for case, bias, low in cases:

                def step(index, carry, bias=bias, low=low):
                    self.add(state_refs, large, index, [*nearer, bias], low)
                    return carry

                lax.fori_loop(zero, jnp.where(case, whole, zero), step, 0)

            def rest(index, carry):
                self.add(state_refs, small, index, self.bias_refs[:count])
                return carry

            lax.fori_loop(whole * (large // small), jnp.where(wanted, end, zero), rest, 0)


def finish(sizes, tile_pos, index, state_refs, weight_ref, out_ref, partial_ref):
    rows, heads, group, dim = sizes
    per_pos = heads * group
    tile = tile_pos * per_pos
    start = pl.multiple_of(index * tile, tile)
    total = jnp.sum(state_refs[1][pl.ds(start, tile), :], axis=1, keepdims=True)
    attended = (state_refs[2][pl.ds(start, tile), :] * (1.0 / total)).astype(jnp.bfloat16)
    out_ref[pl.ds(start, tile), :] = attended
    weight = weight_ref[...].astype(jnp.float32)
    product = attended.astype(jnp.float32).reshape(tile_pos, per_pos, dim) * weight
    partial_ref[pl.ds(pl.multiple_of(index * tile_pos, tile_pos), tile_pos), :] = jnp.sum(product, axis=1)


def tile_copy(sizes, tile_pos, index, out_ref, out_hbm, sem):
    tile = tile_pos * sizes[1] * sizes[2]
    at = pl.ds(pl.multiple_of(index * tile, tile), tile)
    return pltpu.make_async_copy(out_ref.at[at, :], out_hbm.at[at, :], sem)


def add_kernel(sizes, tiles, distances, counts, picks, *refs):
    refs, scratch = refs[: -sum_scratch(counts)], refs[-sum_scratch(counts) :]
    blocks = Blocks(sizes, distances, counts, picks, [*refs, scratch])
    blocks.add_all(blocks.rest[:3], *tiles)


def sum_scratch(counts):
    return len(counts) + sum(n > 1 for n in counts)


def finish_kernel(sizes, tiles, distances, counts, picks, *refs):
    refs, scratch = refs[: -sum_scratch(counts)], refs[-sum_scratch(counts) :]
    blocks = Blocks(sizes, distances, counts, picks, [*refs, scratch])
    weight_ref, *state_refs = blocks.rest[:4]
    out_hbm, partial_ref, out_ref, sems = blocks.rest[4:]
    blocks.add_all(state_refs, *tiles)
    large = tiles[0]
    copies = []
    for index in range(sizes[0] // large):
        finish(sizes, large, index, state_refs, weight_ref, out_ref, partial_ref)
        copies.append(tile_copy(sizes, large, index, out_ref, out_hbm, sems.at[index]))
        copies[-1].start()
    for copy in copies:
        copy.wait()


def redo_kernel(sizes, tiles, distances, counts, picks, *refs):
    refs, scratch = refs[: -sum_scratch(counts)], refs[-sum_scratch(counts) :]
    blocks = Blocks(sizes, distances, counts, picks, [*refs, scratch], True)
    weight_ref, _, _, *state_refs = blocks.rest[:6]
    out_hbm, partial_ref, score_ref, out_ref, sems = blocks.rest[6:]
    small = tiles[1]
    end = jnp.where(blocks.seen[0], (blocks.reached + small - 1) // small, 0)

    def step(index, carry):
        if blocks.middle:

            @pl.when(blocks.upper[0])
            def _():
                blocks.add(state_refs, small, index, blocks.bias_refs, blocks.middle)

        @pl.when(jnp.logical_not(blocks.upper[0]))
        def _():
            blocks.add(state_refs, small, index, blocks.bias_refs)

        finish(sizes, small, index, state_refs, weight_ref, out_ref, partial_ref)
        tile_copy(sizes, small, index, out_ref, out_hbm, sems.at[index]).start()
        return carry

    lax.fori_loop(0, end, step, 0)
    score_ref[...] = lax.dot_general(
        jnp.ones((8, sizes[3]), jnp.float32),
        partial_ref[...],
        (((1,), (1,)), ((), ())),
        preferred_element_type=jnp.float32,
        precision=lax.Precision.HIGHEST,
    )

    def wait(index, carry):
        tile_copy(sizes, small, index, out_ref, out_hbm, sems.at[index]).wait()
        return carry

    lax.fori_loop(0, end, wait, 0)


def call(kernel, sizes, blocks, in_specs, out_specs, out_shape, scratch, aliases, operands):
    rows, heads, group, dim = sizes
    work = 4 * rows * heads * group * dim * rows * blocks
    return pl.pallas_call(
        kernel,
        out_shape=out_shape,
        in_specs=in_specs,
        out_specs=out_specs,
        scratch_shapes=scratch,
        input_output_aliases=aliases,
        cost_estimate=pl.CostEstimate(
            flops=work, bytes_accessed=rows * heads * group * dim * 8, transcendentals=work // (4 * dim)
        ),
        compiler_params=pltpu.CompilerParams(vmem_limit_bytes=32 * 1024 * 1024),
    )(*operands)


def tile_sizes(sizes):
    return math.gcd(sizes[0], 128), math.gcd(sizes[0], 64)


def attend_own(sizes, query, own):
    rows, heads, group, dim = sizes
    flat = (rows * heads * group, dim)
    large = tile_sizes(sizes)[0]
    return call(
        functools.partial(own_kernel, sizes, large),
        sizes,
        1,
        [HBM, VMEM],
        [VMEM] * 4,
        [jax.ShapeDtypeStruct(flat, jnp.bfloat16)] + [jax.ShapeDtypeStruct(flat, jnp.float32)] * 3,
        [pltpu.VMEM((rows, rows), jnp.float32), pltpu.SemaphoreType.DMA((rows // large,))],
        {},
        (pltpu.with_memory_space_constraint(query, pltpu.HBM), own),
    )


def attend_blocks(kernel, sizes, distances, query, own, choices, state, *more):
    rows, heads, group, dim = sizes
    flat = (rows * heads * group, dim)
    tiles = tile_sizes(sizes)
    arrays, picks = [either for either, _ in choices], [pick for _, pick in choices]
    counts = [len(either) for either in arrays]
    operands = [query, own, *sum(arrays, []), *state, *more]
    in_specs = [VMEM] * len(operands)
    at = 2 + sum(counts)
    aliases = {at + n: n for n in range(3)}
    out_shape = [jax.ShapeDtypeStruct(flat, jnp.float32)] * 3
    out_specs = [VMEM] * 3
    scratch = []
    if more:
        out_shape += [pltpu.HBM(flat, jnp.bfloat16), jax.ShapeDtypeStruct((rows, dim), jnp.float32)]
        out_specs += [HBM, VMEM]
        if len(more) > 1:
            in_specs[at + 4] = HBM
            aliases |= {at + 4: 3, at + 5: 4}
            out_shape.append(jax.ShapeDtypeStruct((8, rows), jnp.float32))
            out_specs.append(VMEM)
        scratch += [pltpu.VMEM(flat, jnp.bfloat16), pltpu.SemaphoreType.DMA((rows // tiles[1],))]
    scratch += [pltpu.VMEM((rows, rows), jnp.float32)] * len(choices)
    scratch += [pltpu.VMEM(own.shape, own.dtype) for n in counts if n > 1]
    outs = call(
        functools.partial(kernel, sizes, tiles, distances, counts, picks),
        sizes,
        len(choices),
        in_specs,
        out_specs,
        out_shape,
        scratch,
        aliases,
        operands,
    )
    return outs[:3], outs[3:]


def local(groups, devices, queries, keys, values, segments, score_weight):
    rows, heads, group, dim = queries.shape
    reach = rows * devices // 2
    back = min(devices - 1, -(-(reach - 1) // rows))
    sizes = (rows, heads, group, dim)

    def send(array, pairs):
        return lax.ppermute(array, "ctx", [(s, t) for s, t in pairs if t < devices])

    def send_whole(array, pairs):
        pairs = [(s, t) for s, t in pairs if t < devices]
        return lax.ppermute(array, ("groups", "ctx"), whole_permutation(pairs, groups, devices))

    weight = score_weight.reshape(heads * group, dim)
    own = pack(keys, values, segments)
    swap = [(i, i ^ 1) for i in range(devices)]
    if devices % 4 == 0:
        gap = devices // 2
        around = {i: (i + 1) % devices for i in range(devices)} | {gap: 0, devices - 1: gap + 1}
        near = ([send(own, around.items()), send(own, swap)], lambda place: jnp.where(place == gap + 1, 1, 0))
    else:
        near = ([send(own, [(i, i + 1) for i in range(devices)])], None)
    far = [send(own, [(i, i + 2) for i in range(parity, devices, 2)]) for parity in range(2)]
    by_parity = lambda place: place % 2
    query, *state = attend_own(sizes, queries.reshape(rows * heads * group, dim), own)
    relayed, query = lax.optimization_barrier((near[0][0], query))
    for distance in range(1, back + 1, 2):
        step = [near, (far, by_parity)][: back + 1 - distance]
        if distance + 2 <= back:
            relayed = send_whole(relayed, [(i, i + 2) for i in range(0, devices, 2)])
            next_near = ([relayed, send(far[0], swap)], by_parity)
            if distance + 3 <= back:
                starts = range(distance + 1, devices, 2), range(distance + 2, devices, 2)
                ways = [[(i, i + 2) for i in start] for start in starts]
                far = [send(far[0], ways[0]), send_whole(far[1], ways[1])]
            state, _ = attend_blocks(add_kernel, sizes, (distance, distance + 1), query, own, step, state)
            near = next_near
    state, outs = attend_blocks(finish_kernel, sizes, (distance,), query, own, step[:1], state, weight)
    if len(step) == 1:
        distance, step = devices, step * 2
    _, outs = attend_blocks(redo_kernel, sizes, (distance + 1,), query, own, step[1:], state, weight, *outs)
    attended, _, score = outs
    score = score[0]
    score = score + lax.ppermute(score, "head", [(0, 1), (1, 0)])
    return attended.reshape(queries.shape), score


def solution(mesh):
    return jax.shard_map(
        functools.partial(local, mesh.shape["groups"], mesh.shape["ctx"]),
        mesh=mesh,
        in_specs=(
            P(("groups", "ctx"), "head", None, None),
            P(("groups", "ctx"), "head", None),
            P(("groups", "ctx"), "head", None),
            P(("groups", "ctx")),
            P("head", None, None),
        ),
        out_specs=(P(("groups", "ctx"), "head", None, None), P(("groups", "ctx"))),
        check_vma=False,
    )
```

```python
import functools
import math

import jax
import jax.numpy as jnp
from jax import lax
from jax.experimental import pallas as pl
from jax.experimental.pallas import tpu as pltpu
from jax.sharding import PartitionSpec as P

HIDDEN = -1e30
LABEL_ROWS = 16
LANES = 128
VMEM = pl.BlockSpec(memory_space=pltpu.VMEM)
HBM = pl.BlockSpec(memory_space=pltpu.HBM)


def whole_permutation(pairs, groups, devices):
    onward = dict(pairs)
    targets = set(onward.values())
    ends = {}
    for start in onward.keys() - targets:
        end = start
        while end in onward:
            end = onward[end]
        ends[end] = start
    idle = [i for i in range(devices) if i not in onward and i not in targets] if groups > 1 else []
    return [
        (g * devices + s, g * devices + t) for g in range(groups) for s, t in sorted({**onward, **ends}.items())
    ] + [(g * devices + i, (g + 1) % groups * devices + i) for g in range(groups) for i in idle]


def pack_kernel(key_hbm, value_hbm, seg_hbm, out_ref, key_ref, value_ref, seg_ref, sems):
    copies = [
        pltpu.make_async_copy(source, target, sems.at[n])
        for n, (source, target) in enumerate(((key_hbm, key_ref), (value_hbm, value_ref), (seg_hbm, seg_ref)))
    ]
    for copy in copies:
        copy.start()
    rows, heads, dim = key_ref.shape
    for n, ref in enumerate((key_ref, value_ref)):
        copies[n].wait()
        for h in range(heads):
            out_ref[n * rows : (n + 1) * rows, h * dim : (h + 1) * dim] = ref[:, h, :]
    copies[2].wait()
    labels = (seg_ref[...] + 1).astype(jnp.float32).astype(jnp.bfloat16)
    empty = jnp.zeros((out_ref.shape[0] - 2 * rows - labels.shape[0], labels.shape[1]), jnp.bfloat16)
    out_ref[2 * rows :, :] = jnp.concatenate([labels, empty], axis=0)


def pack(keys, values, segments):
    rows, heads, dim = keys.shape
    lanes = heads * dim
    lines = -(-rows // lanes)
    segments = jnp.pad(segments, (0, lines * lanes - rows), constant_values=-1).reshape(lines, lanes)
    return pl.pallas_call(
        pack_kernel,
        out_shape=jax.ShapeDtypeStruct((2 * rows + lines + -lines % LABEL_ROWS, lanes), keys.dtype),
        in_specs=[HBM] * 3,
        out_specs=VMEM,
        scratch_shapes=[
            pltpu.VMEM(keys.shape, keys.dtype),
            pltpu.VMEM(values.shape, values.dtype),
            pltpu.VMEM(segments.shape, segments.dtype),
            pltpu.SemaphoreType.DMA((3,)),
        ],
        compiler_params=pltpu.CompilerParams(vmem_limit_bytes=4 * 1024 * 1024),
    )(*(pltpu.with_memory_space_constraint(x, pltpu.HBM) for x in (keys, values, segments)))


def labels_of(ref, rows):
    lines = -(-rows // ref.shape[1])
    grid = ref[2 * rows :, :].astype(jnp.float32)
    return jnp.concatenate([grid[n : n + 1, :] for n in range(lines)], axis=1)[:, :rows]


def fill_bias(bias_ref, labels, own, causal):
    rows = bias_ref.shape[0]
    own_column = jnp.transpose(jnp.broadcast_to(own, (LANES, rows)))[:, :1]
    seen = labels == own_column
    if causal:
        key = lax.broadcasted_iota(jnp.int32, (rows, rows), 1)
        seen = seen & (key <= lax.broadcasted_iota(jnp.int32, (rows, rows), 0))
    bias_ref[...] = jnp.where(seen, 0.0, HIDDEN)


def update(sizes, tile_pos, index, fresh, reached, query_ref, blocks, state_refs):
    rows, heads, group, dim = sizes
    scale = math.log2(math.e) / math.sqrt(dim)
    tile, half = tile_pos * heads * group, tile_pos * group
    start = pl.multiple_of(index * tile, tile)
    query = query_ref[pl.ds(start, tile), :].astype(jnp.float32).reshape(tile_pos, heads, group, dim)
    biases = []
    for _, bias, low, high in blocks:
        if bias is None:
            biases.append(None)
        elif isinstance(bias, jax.Array):
            biases.append(jnp.broadcast_to(bias[:, low:high], (half, high - low)))
        else:
            lines = [bias[pl.ds(index * tile_pos + p, 1), :][:, low:high] for p in range(tile_pos)]
            biases.append(jnp.concatenate([jnp.broadcast_to(line, (group, high - low)) for line in lines], axis=0))
    if not fresh:
        old_states = [ref[pl.ds(start, tile), :].reshape(tile_pos, heads, group, dim) for ref in state_refs]
    if reached is not None:
        row = lax.broadcasted_iota(jnp.int32, (half, dim), 0)
        changed = row < (reached - index * tile_pos) * group
    outs = [], [], []
    for h in range(heads):
        at = slice(h * dim, (h + 1) * dim)
        query_h = query[:, h].reshape(half, dim).astype(jnp.bfloat16)
        scores = []
        for (block_ref, _, low, high), bias in zip(blocks, biases):
            score = lax.dot_general(
                query_h, block_ref[low:high, at], (((1,), (1,)), ((), ())), preferred_element_type=jnp.float32
            )
            if bias is not None:
                score = score + bias
            scores.append([score[:, c : c + LANES] for c in range(0, high - low, LANES)])
        old = [] if fresh else [state[:, h].reshape(half, dim) for state in old_states]
        top = jnp.max(functools.reduce(jnp.maximum, sum(scores, old[:1])), axis=1, keepdims=True)
        weights = [[jnp.exp2((part - top) * scale) for part in parts] for parts in scores]
        total = functools.reduce(jnp.add, sum(weights, []))
        acc = None
        for (block_ref, _, low, high), parts in zip(blocks, weights):
            rounded = jnp.concatenate([part.astype(jnp.bfloat16) for part in parts], axis=1)
            part = jnp.dot(rounded, block_ref[rows + low : rows + high, at], preferred_element_type=jnp.float32)
            acc = part if acc is None else acc + part
        if not fresh:
            factor = jnp.exp2((old[0] - top) * scale)
            total = total + old[1] * factor
            acc = acc + old[2] * factor
        new = [jnp.broadcast_to(top, acc.shape), total, acc]
        if reached is not None:
            new = [jnp.where(changed, part, kept) for part, kept in zip(new, old)]
        for out, part in zip(outs, new):
            out.append(part.reshape(tile_pos, 1, group, dim))
    for ref, parts in zip(state_refs, outs):
        ref[pl.ds(start, tile), :] = jnp.concatenate(parts, axis=1).reshape(tile, dim)


def own_kernel(sizes, tile_pos, query_hbm, block_ref, query_ref, *refs):
    *state_refs, bias_ref, sems = refs
    rows, heads, group, _ = sizes
    tile = tile_pos * heads * group
    copies = [
        pltpu.make_async_copy(
            query_hbm.at[pl.ds(n * tile, tile), :], query_ref.at[pl.ds(n * tile, tile), :], sems.at[n]
        )
        for n in range(rows // tile_pos)
    ]
    for copy in copies:
        copy.start()
    own = labels_of(block_ref, rows)
    fill_bias(bias_ref, own, own, True)
    for n, copy in enumerate(copies):
        copy.wait()
        high = min(rows, -(-((n + 1) * tile_pos) // LANES) * LANES)
        update(sizes, tile_pos, n, True, None, query_ref, [(block_ref, bias_ref, 0, high)], state_refs)


class Blocks:
    def __init__(self, sizes, tile_pos, distances, counts, picks, refs):
        self.sizes, self.tile_pos = sizes, tile_pos
        rows = sizes[0]
        refs = list(refs)
        self.query_ref, own_ref = refs.pop(0), refs.pop(0)
        either_refs = [[refs.pop(0) for _ in range(n)] for n in counts]
        del refs[:3]
        copies = [refs.pop() for n in counts if n > 1]
        self.rest = refs
        place = lax.axis_index("ctx")
        self.block_refs = []
        for either, pick in zip(either_refs, picks):
            self.block_refs.append(either[0] if len(either) == 1 else copies.pop())
            if len(either) > 1:
                for n, ref in enumerate(either):

                    @pl.when(pick(place) == n)
                    def _(ref=ref, block_ref=self.block_refs[-1]):
                        block_ref[...] = ref[...]

        own = labels_of(own_ref, rows)
        first_label = jnp.min(own)
        self.reached = jnp.sum(jnp.where(own == first_label, 1.0, 0.0)).astype(jnp.int32)
        self.tiles_reached = (self.reached + tile_pos - 1) // tile_pos
        labels = [labels_of(ref, rows) for ref in self.block_refs]
        self.seen = [(jnp.max(label) == first_label) & (place >= far) for label, far in zip(labels, distances)]
        self.full = [see & (jnp.min(label) == first_label) for label, see in zip(labels, self.seen)]
        self.middle = rows // 2 // LANES * LANES
        self.upper = [
            jnp.max(label[:, : self.middle]) < first_label if self.middle else jnp.bool_(False) for label in labels
        ]
        self.key_bias = [jnp.where(label == first_label, 0.0, HIDDEN) for label in labels]

    def add(self, state_refs, index, biases, low=0):
        blocks = [(self.block_refs[n], bias, low, self.sizes[0]) for n, bias in enumerate(biases)]
        update(self.sizes, self.tile_pos, index, False, self.reached, self.query_ref, blocks, state_refs)

    def cases(self):
        many = len(self.seen)
        cases = []
        for count in range(1, many + 1):
            wanted = self.seen[count - 1]
            if count < many:
                wanted = wanted & jnp.logical_not(self.seen[count])
            nearer, bias = [None] * (count - 1), self.key_bias[count - 1]
            full, upper = self.full[count - 1], self.upper[count - 1]
            if count < many:
                cases.append((wanted, [*nearer, bias], 0))
                continue
            cases.append((wanted & full, [*nearer, None], 0))
            if many == 1 and self.middle:
                cases.append((wanted & upper, [bias], self.middle))
                wanted = wanted & jnp.logical_not(upper)
            cases.append((wanted & jnp.logical_not(full), [*nearer, bias], 0))
        return cases

    def add_all(self, state_refs):
        for wanted, biases, low in self.cases():

            def step(index, carry, biases=biases, low=low):
                self.add(state_refs, index, biases, low)
                return carry

            lax.fori_loop(0, jnp.where(wanted, self.tiles_reached, 0), step, 0)


def finish(sizes, tile_pos, index, state_refs, weight_ref, out_ref, partial_ref):
    rows, heads, group, dim = sizes
    per_pos = heads * group
    tile = tile_pos * per_pos
    start = pl.multiple_of(index * tile, tile)
    total = jnp.sum(state_refs[1][pl.ds(start, tile), :], axis=1, keepdims=True)
    attended = (state_refs[2][pl.ds(start, tile), :] * (1.0 / total)).astype(jnp.bfloat16)
    out_ref[pl.ds(start, tile), :] = attended
    weight = weight_ref[...].astype(jnp.float32)
    product = attended.astype(jnp.float32).reshape(tile_pos, per_pos, dim) * weight
    partial_ref[pl.ds(pl.multiple_of(index * tile_pos, tile_pos), tile_pos), :] = jnp.sum(product, axis=1)


def tile_copy(sizes, tile_pos, index, out_ref, out_hbm, sem):
    tile = tile_pos * sizes[1] * sizes[2]
    at = pl.ds(pl.multiple_of(index * tile, tile), tile)
    return pltpu.make_async_copy(out_ref.at[at, :], out_hbm.at[at, :], sem)


def add_kernel(sizes, tile_pos, distances, counts, picks, *refs):
    blocks = Blocks(sizes, tile_pos, distances, counts, picks, refs)
    blocks.add_all(blocks.rest[:3])


def finish_kernel(sizes, tile_pos, distances, counts, picks, *refs):
    blocks = Blocks(sizes, tile_pos, distances, counts, picks, refs)
    weight_ref, *state_refs = blocks.rest[:4]
    out_hbm, partial_ref, open_ref, out_ref, sems = blocks.rest[4:]
    blocks.add_all(state_refs)
    opened = jnp.where(blocks.full[0] & (blocks.reached < sizes[0]), blocks.tiles_reached, 0)
    open_ref[...] = jnp.broadcast_to(opened.astype(jnp.float32), open_ref.shape)
    tiles = sizes[0] // tile_pos
    for index in range(tiles):

        @pl.when(index >= opened)
        def _(index=index):
            finish(sizes, tile_pos, index, state_refs, weight_ref, out_ref, partial_ref)
            tile_copy(sizes, tile_pos, index, out_ref, out_hbm, sems.at[index]).start()

    for index in range(tiles):

        @pl.when(index >= opened)
        def _(index=index):
            tile_copy(sizes, tile_pos, index, out_ref, out_hbm, sems.at[index]).wait()


def redo_kernel(sizes, tile_pos, distances, counts, picks, *refs):
    blocks = Blocks(sizes, tile_pos, distances, counts, picks, refs)
    weight_ref, _, _, open_ref, *state_refs = blocks.rest[:7]
    out_hbm, partial_ref, score_ref, out_ref, sems = blocks.rest[7:]
    opened = jnp.max(open_ref[...]).astype(jnp.int32)

    for wanted, biases, low in blocks.cases() + [(jnp.logical_not(blocks.seen[0]), None, 0)]:

        def step(index, carry, biases=biases, low=low):
            if biases is not None:
                blocks.add(state_refs, index, biases, low)
            finish(sizes, tile_pos, index, state_refs, weight_ref, out_ref, partial_ref)
            tile_copy(sizes, tile_pos, index, out_ref, out_hbm, sems.at[index]).start()
            return carry

        lax.fori_loop(0, jnp.where(wanted, opened, 0), step, 0)

    score_ref[...] = lax.dot_general(
        jnp.ones((8, sizes[3]), jnp.float32),
        partial_ref[...],
        (((1,), (1,)), ((), ())),
        preferred_element_type=jnp.float32,
        precision=lax.Precision.HIGHEST,
    )

    def wait(index, carry):
        tile_copy(sizes, tile_pos, index, out_ref, out_hbm, sems.at[index]).wait()
        return carry

    lax.fori_loop(0, opened, wait, 0)


def call(kernel, sizes, blocks, in_specs, out_specs, out_shape, scratch, aliases, operands):
    rows, heads, group, dim = sizes
    work = 4 * rows * heads * group * dim * rows * blocks
    return pl.pallas_call(
        kernel,
        out_shape=out_shape,
        in_specs=in_specs,
        out_specs=out_specs,
        scratch_shapes=scratch,
        input_output_aliases=aliases,
        cost_estimate=pl.CostEstimate(
            flops=work, bytes_accessed=rows * heads * group * dim * 8, transcendentals=work // (4 * dim)
        ),
        compiler_params=pltpu.CompilerParams(vmem_limit_bytes=32 * 1024 * 1024),
    )(*operands)


def attend_own(sizes, query, own):
    rows, heads, group, dim = sizes
    flat = (rows * heads * group, dim)
    tile_pos = math.gcd(rows, 128)
    return call(
        functools.partial(own_kernel, sizes, tile_pos),
        sizes,
        1,
        [HBM, VMEM],
        [VMEM] * 4,
        [jax.ShapeDtypeStruct(flat, jnp.bfloat16)] + [jax.ShapeDtypeStruct(flat, jnp.float32)] * 3,
        [pltpu.VMEM((rows, rows), jnp.float32), pltpu.SemaphoreType.DMA((rows // tile_pos,))],
        {},
        (pltpu.with_memory_space_constraint(query, pltpu.HBM), own),
    )


def attend_blocks(kernel, sizes, distances, query, own, choices, state, *more):
    rows, heads, group, dim = sizes
    flat = (rows * heads * group, dim)
    tile_pos = math.gcd(rows, 128)
    arrays, picks = [either for either, _ in choices], [pick for _, pick in choices]
    counts = [len(either) for either in arrays]
    operands = [query, own, *sum(arrays, []), *state, *more]
    in_specs = [VMEM] * len(operands)
    at = 2 + sum(counts)
    aliases = {at + n: n for n in range(3)}
    out_shape = [jax.ShapeDtypeStruct(flat, jnp.float32)] * 3
    out_specs = [VMEM] * 3
    scratch = []
    if more:
        again = len(more) > 1
        out_shape += [pltpu.HBM(flat, jnp.bfloat16), jax.ShapeDtypeStruct((rows, dim), jnp.float32)]
        out_shape.append(jax.ShapeDtypeStruct((8, rows if again else LANES), jnp.float32))
        out_specs += [HBM, VMEM, VMEM]
        if again:
            in_specs[at + 4] = HBM
            aliases |= {at + 4: 3, at + 5: 4}
        scratch += [pltpu.VMEM(flat, jnp.bfloat16), pltpu.SemaphoreType.DMA((rows // tile_pos,))]
    scratch += [pltpu.VMEM(own.shape, own.dtype) for n in counts if n > 1]
    outs = call(
        functools.partial(kernel, sizes, tile_pos, distances, counts, picks),
        sizes,
        len(choices),
        in_specs,
        out_specs,
        out_shape,
        scratch,
        aliases,
        operands,
    )
    return outs[:3], outs[3:]


def local(groups, devices, queries, keys, values, segments, score_weight):
    rows, heads, group, dim = queries.shape
    reach = rows * devices // 2
    back = min(devices - 1, -(-(reach - 1) // rows))
    sizes = (rows, heads, group, dim)

    def send(array, pairs):
        return lax.ppermute(array, "ctx", [(s, t) for s, t in pairs if t < devices])

    def send_whole(array, pairs):
        pairs = [(s, t) for s, t in pairs if t < devices]
        return lax.ppermute(array, ("groups", "ctx"), whole_permutation(pairs, groups, devices))

    weight = score_weight.reshape(heads * group, dim)
    own = pack(keys, values, segments)
    swap = [(i, i ^ 1) for i in range(devices)]
    if devices % 4 == 0:
        gap = devices // 2
        around = {i: (i + 1) % devices for i in range(devices)} | {gap: 0, devices - 1: gap + 1}
        near = ([send(own, around.items()), send(own, swap)], lambda place: jnp.where(place == gap + 1, 1, 0))
    else:
        near = ([send(own, [(i, i + 1) for i in range(devices)])], None)
    far = [send(own, [(i, i + 2) for i in range(parity, devices, 2)]) for parity in range(2)]
    by_parity = lambda place: place % 2
    query, *state = attend_own(sizes, queries.reshape(rows * heads * group, dim), own)
    relayed, query = lax.optimization_barrier((near[0][0], query))
    for distance in range(1, back + 1, 2):
        step = [near, (far, by_parity)][: back + 1 - distance]
        if distance + 2 <= back:
            relayed = send_whole(relayed, [(i, i + 2) for i in range(0, devices, 2)])
            next_near = ([relayed, send(far[0], swap)], by_parity)
            if distance + 3 <= back:
                starts = range(distance + 1, devices, 2), range(distance + 2, devices, 2)
                ways = [[(i, i + 2) for i in start] for start in starts]
                far = [send(far[0], ways[0]), send_whole(far[1], ways[1])]
            state, _ = attend_blocks(add_kernel, sizes, (distance, distance + 1), query, own, step, state)
            near = next_near
    state, outs = attend_blocks(finish_kernel, sizes, (distance,), query, own, step[:1], state, weight)
    if len(step) == 1:
        distance, step = devices, step * 2
    _, outs = attend_blocks(redo_kernel, sizes, (distance + 1,), query, own, step[1:], state, weight, *outs)
    attended, _, score = outs
    score = score[0]
    score = score + lax.ppermute(score, "head", [(0, 1), (1, 0)])
    return attended.reshape(queries.shape), score


def solution(mesh):
    return jax.shard_map(
        functools.partial(local, mesh.shape["groups"], mesh.shape["ctx"]),
        mesh=mesh,
        in_specs=(
            P(("groups", "ctx"), "head", None, None),
            P(("groups", "ctx"), "head", None),
            P(("groups", "ctx"), "head", None),
            P(("groups", "ctx")),
            P("head", None, None),
        ),
        out_specs=(P(("groups", "ctx"), "head", None, None), P(("groups", "ctx"))),
        check_vma=False,
    )
```

```python
import functools
import math

import jax
import jax.numpy as jnp
from jax import lax
from jax.experimental import pallas as pl
from jax.experimental.pallas import tpu as pltpu
from jax.sharding import PartitionSpec as P

HIDDEN = -1e30
LABEL_ROWS = 16
LANES = 128
VMEM = pl.BlockSpec(memory_space=pltpu.VMEM)
HBM = pl.BlockSpec(memory_space=pltpu.HBM)


def whole_permutation(pairs, groups, devices):
    onward = dict(pairs)
    targets = set(onward.values())
    ends = {}
    for start in onward.keys() - targets:
        end = start
        while end in onward:
            end = onward[end]
        ends[end] = start
    idle = [i for i in range(devices) if i not in onward and i not in targets] if groups > 1 else []
    return [
        (g * devices + s, g * devices + t) for g in range(groups) for s, t in sorted({**onward, **ends}.items())
    ] + [(g * devices + i, (g + 1) % groups * devices + i) for g in range(groups) for i in idle]


def pack_kernel(key_hbm, value_hbm, seg_hbm, out_ref, key_ref, value_ref, seg_ref, sems):
    copies = [
        pltpu.make_async_copy(source, target, sems.at[n])
        for n, (source, target) in enumerate(((key_hbm, key_ref), (value_hbm, value_ref), (seg_hbm, seg_ref)))
    ]
    for copy in copies:
        copy.start()
    rows, heads, dim = key_ref.shape
    for n, ref in enumerate((key_ref, value_ref)):
        copies[n].wait()
        for h in range(heads):
            out_ref[n * rows : (n + 1) * rows, h * dim : (h + 1) * dim] = ref[:, h, :]
    copies[2].wait()
    labels = (seg_ref[...] + 1).astype(jnp.float32).astype(jnp.bfloat16)
    empty = jnp.zeros((out_ref.shape[0] - 2 * rows - labels.shape[0], labels.shape[1]), jnp.bfloat16)
    out_ref[2 * rows :, :] = jnp.concatenate([labels, empty], axis=0)


def pack(keys, values, segments):
    rows, heads, dim = keys.shape
    lanes = heads * dim
    lines = -(-rows // lanes)
    segments = jnp.pad(segments, (0, lines * lanes - rows), constant_values=-1).reshape(lines, lanes)
    return pl.pallas_call(
        pack_kernel,
        out_shape=jax.ShapeDtypeStruct((2 * rows + lines + -lines % LABEL_ROWS, lanes), keys.dtype),
        in_specs=[HBM] * 3,
        out_specs=VMEM,
        scratch_shapes=[
            pltpu.VMEM(keys.shape, keys.dtype),
            pltpu.VMEM(values.shape, values.dtype),
            pltpu.VMEM(segments.shape, segments.dtype),
            pltpu.SemaphoreType.DMA((3,)),
        ],
        compiler_params=pltpu.CompilerParams(vmem_limit_bytes=4 * 1024 * 1024),
    )(*(pltpu.with_memory_space_constraint(x, pltpu.HBM) for x in (keys, values, segments)))


def labels_of(ref, rows):
    lines = -(-rows // ref.shape[1])
    grid = ref[2 * rows :, :].astype(jnp.float32)
    return jnp.concatenate([grid[n : n + 1, :] for n in range(lines)], axis=1)[:, :rows]


def fill_bias(bias_ref, labels, own, causal):
    rows = bias_ref.shape[0]
    own_column = jnp.transpose(jnp.broadcast_to(own, (LANES, rows)))[:, :1]
    seen = labels == own_column
    if causal:
        key = lax.broadcasted_iota(jnp.int32, (rows, rows), 1)
        seen = seen & (key <= lax.broadcasted_iota(jnp.int32, (rows, rows), 0))
    bias_ref[...] = jnp.where(seen, 0.0, HIDDEN)


def update(sizes, tile_pos, index, fresh, reached, query_ref, blocks, state_refs):
    rows, heads, group, dim = sizes
    scale = math.log2(math.e) / math.sqrt(dim)
    tile, half = tile_pos * heads * group, tile_pos * group
    start = pl.multiple_of(index * tile, tile)
    query = query_ref[pl.ds(start, tile), :].astype(jnp.float32).reshape(tile_pos, heads, group, dim)
    biases = []
    for _, bias, low, high in blocks:
        if bias is None:
            biases.append(None)
        elif isinstance(bias, jax.Array):
            biases.append(jnp.broadcast_to(bias[:, low:high], (half, high - low)))
        else:
            lines = [bias[pl.ds(index * tile_pos + p, 1), :][:, low:high] for p in range(tile_pos)]
            biases.append(jnp.concatenate([jnp.broadcast_to(line, (group, high - low)) for line in lines], axis=0))
    if not fresh:
        old_states = [ref[pl.ds(start, tile), :].reshape(tile_pos, heads, group, dim) for ref in state_refs]
    if reached is not None:
        row = lax.broadcasted_iota(jnp.int32, (half, dim), 0)
        changed = row < (reached - index * tile_pos) * group
    outs = [], [], []
    for h in range(heads):
        at = slice(h * dim, (h + 1) * dim)
        query_h = query[:, h].reshape(half, dim).astype(jnp.bfloat16)
        scores = []
        for (block_ref, _, low, high), bias in zip(blocks, biases):
            score = lax.dot_general(
                query_h, block_ref[low:high, at], (((1,), (1,)), ((), ())), preferred_element_type=jnp.float32
            )
            if bias is not None:
                score = score + bias
            scores.append([score[:, c : c + LANES] for c in range(0, high - low, LANES)])
        old = [] if fresh else [state[:, h].reshape(half, dim) for state in old_states]
        top = jnp.max(functools.reduce(jnp.maximum, sum(scores, old[:1])), axis=1, keepdims=True)
        weights = [[jnp.exp2((part - top) * scale) for part in parts] for parts in scores]
        total = functools.reduce(jnp.add, sum(weights, []))
        acc = None
        for (block_ref, _, low, high), parts in zip(blocks, weights):
            rounded = jnp.concatenate([part.astype(jnp.bfloat16) for part in parts], axis=1)
            part = jnp.dot(rounded, block_ref[rows + low : rows + high, at], preferred_element_type=jnp.float32)
            acc = part if acc is None else acc + part
        if not fresh:
            factor = jnp.exp2((old[0] - top) * scale)
            total = total + old[1] * factor
            acc = acc + old[2] * factor
        new = [jnp.broadcast_to(top, acc.shape), total, acc]
        if reached is not None:
            new = [jnp.where(changed, part, kept) for part, kept in zip(new, old)]
        for out, part in zip(outs, new):
            out.append(part.reshape(tile_pos, 1, group, dim))
    for ref, parts in zip(state_refs, outs):
        ref[pl.ds(start, tile), :] = jnp.concatenate(parts, axis=1).reshape(tile, dim)


def own_kernel(sizes, tile_pos, query_hbm, block_ref, query_ref, *refs):
    *state_refs, bias_ref, sems = refs
    rows, heads, group, _ = sizes
    tile = tile_pos * heads * group
    copies = [
        pltpu.make_async_copy(
            query_hbm.at[pl.ds(n * tile, tile), :], query_ref.at[pl.ds(n * tile, tile), :], sems.at[n]
        )
        for n in range(rows // tile_pos)
    ]
    for copy in copies:
        copy.start()
    own = labels_of(block_ref, rows)
    fill_bias(bias_ref, own, own, True)
    for n, copy in enumerate(copies):
        copy.wait()
        high = min(rows, -(-((n + 1) * tile_pos) // LANES) * LANES)
        update(sizes, tile_pos, n, True, None, query_ref, [(block_ref, bias_ref, 0, high)], state_refs)


class Blocks:
    def __init__(self, sizes, tile_pos, distances, counts, picks, refs):
        self.sizes, self.tile_pos = sizes, tile_pos
        rows = sizes[0]
        refs = list(refs)
        self.query_ref, own_ref = refs.pop(0), refs.pop(0)
        either_refs = [[refs.pop(0) for _ in range(n)] for n in counts]
        del refs[:3]
        copies = [refs.pop() for n in counts if n > 1]
        self.rest = refs
        place = lax.axis_index("ctx")
        self.block_refs = []
        for either, pick in zip(either_refs, picks):
            self.block_refs.append(either[0] if len(either) == 1 else copies.pop())
            if len(either) > 1:
                for n, ref in enumerate(either):

                    @pl.when(pick(place) == n)
                    def _(ref=ref, block_ref=self.block_refs[-1]):
                        block_ref[...] = ref[...]

        own = labels_of(own_ref, rows)
        first_label = jnp.min(own)
        self.reached = jnp.sum(jnp.where(own == first_label, 1.0, 0.0)).astype(jnp.int32)
        self.tiles_reached = (self.reached + tile_pos - 1) // tile_pos
        labels = [labels_of(ref, rows) for ref in self.block_refs]
        self.seen = [(jnp.max(label) == first_label) & (place >= far) for label, far in zip(labels, distances)]
        self.full = [see & (jnp.min(label) == first_label) for label, see in zip(labels, self.seen)]
        self.middle = rows // 2 // LANES * LANES
        self.upper = [
            jnp.max(label[:, : self.middle]) < first_label if self.middle else jnp.bool_(False) for label in labels
        ]
        self.key_bias = [jnp.where(label == first_label, 0.0, HIDDEN) for label in labels]

    def add(self, state_refs, index, biases, low=0, reached=None):
        blocks = [(self.block_refs[n], bias, low, self.sizes[0]) for n, bias in enumerate(biases)]
        update(self.sizes, self.tile_pos, index, False, reached, self.query_ref, blocks, state_refs)

    def cases(self):
        many = len(self.seen)
        cases = []
        for count in range(many, 0, -1):
            wanted = self.seen[count - 1]
            if count < many:
                wanted = wanted & jnp.logical_not(self.seen[count])
            nearer, bias = [None] * (count - 1), self.key_bias[count - 1]
            full, upper = self.full[count - 1], self.upper[count - 1]
            if count < many:
                cases.append((wanted, [*nearer, bias], 0))
                continue
            cases.append((wanted & full, [*nearer, None], 0))
            if many == 1 and self.middle:
                cases.append((wanted & upper, [bias], self.middle))
                wanted = wanted & jnp.logical_not(upper)
            cases.append((wanted & jnp.logical_not(full), [*nearer, bias], 0))
        return cases

    def add_all(self, state_refs):
        tiles = self.sizes[0] // self.tile_pos
        (wanted, biases, low), *others = self.cases()
        every = wanted & (self.reached == self.sizes[0])

        @pl.when(every)
        def _():
            for index in range(tiles):
                self.add(state_refs, index, biases, low)

        for wanted, biases, low in [(wanted & jnp.logical_not(every), biases, low), *others]:

            def step(index, carry, biases=biases, low=low):
                self.add(state_refs, index, biases, low, self.reached)
                return carry

            lax.fori_loop(0, jnp.where(wanted, self.tiles_reached, 0), step, 0)


def finish(sizes, tile_pos, index, state_refs, weight_ref, out_ref, partial_ref):
    rows, heads, group, dim = sizes
    per_pos = heads * group
    tile = tile_pos * per_pos
    start = pl.multiple_of(index * tile, tile)
    total = jnp.sum(state_refs[1][pl.ds(start, tile), :], axis=1, keepdims=True)
    attended = (state_refs[2][pl.ds(start, tile), :] * (1.0 / total)).astype(jnp.bfloat16)
    out_ref[pl.ds(start, tile), :] = attended
    weight = weight_ref[...].astype(jnp.float32)
    product = attended.astype(jnp.float32).reshape(tile_pos, per_pos, dim) * weight
    partial_ref[pl.ds(pl.multiple_of(index * tile_pos, tile_pos), tile_pos), :] = jnp.sum(product, axis=1)


def tile_copy(sizes, tile_pos, index, out_ref, out_hbm, sem):
    tile = tile_pos * sizes[1] * sizes[2]
    at = pl.ds(pl.multiple_of(index * tile, tile), tile)
    return pltpu.make_async_copy(out_ref.at[at, :], out_hbm.at[at, :], sem)


def score_of(partial_ref, score_ref):
    score_ref[...] = lax.dot_general(
        jnp.ones((score_ref.shape[0], partial_ref.shape[1]), jnp.float32),
        partial_ref[...],
        (((1,), (1,)), ((), ())),
        preferred_element_type=jnp.float32,
        precision=lax.Precision.HIGHEST,
    )


def add_kernel(sizes, tile_pos, distances, counts, picks, *refs):
    blocks = Blocks(sizes, tile_pos, distances, counts, picks, refs)
    blocks.add_all(blocks.rest[:3])


def finish_kernel(sizes, tile_pos, distances, counts, picks, *refs):
    blocks = Blocks(sizes, tile_pos, distances, counts, picks, refs)
    weight_ref, *state_refs = blocks.rest[:4]
    out_hbm, partial_ref, open_ref, score_ref, out_ref, sems = blocks.rest[4:]
    opened = jnp.where(blocks.full[0] & (blocks.reached < sizes[0]), blocks.tiles_reached, 0)
    open_ref[...] = jnp.broadcast_to(opened.astype(jnp.float32), open_ref.shape)
    tiles = sizes[0] // tile_pos
    cases = blocks.cases()
    all_open = opened == tiles

    @pl.when(all_open)
    def _():
        for index in range(tiles):
            blocks.add(state_refs, index, cases[0][1], cases[0][2], blocks.reached)

    def step(count, carry):
        index = tiles - 1 - count
        for wanted, biases, low in cases:

            @pl.when(wanted & (index < blocks.tiles_reached))
            def _(biases=biases, low=low):
                blocks.add(state_refs, index, biases, low, blocks.reached)

        @pl.when(index >= opened)
        def _():
            finish(sizes, tile_pos, index, state_refs, weight_ref, out_ref, partial_ref)
            tile_copy(sizes, tile_pos, index, out_ref, out_hbm, sems.at[index]).start()

        return carry

    lax.fori_loop(0, jnp.where(all_open, 0, tiles), step, 0)

    @pl.when(opened == 0)
    def _():
        score_of(partial_ref, score_ref)

    for index in range(tiles):

        @pl.when(index >= opened)
        def _(index=index):
            tile_copy(sizes, tile_pos, index, out_ref, out_hbm, sems.at[index]).wait()


def redo_kernel(sizes, tile_pos, distances, counts, picks, *refs):
    at = 2 + sum(counts) + 3
    weight_ref, _, _, open_ref, _ = refs[at : at + 5]
    opened = jnp.max(open_ref[...]).astype(jnp.int32)

    @pl.when(opened > 0)
    def _():
        blocks = Blocks(sizes, tile_pos, distances, counts, picks, refs)
        state_refs = blocks.rest[5:8]
        out_hbm, partial_ref, _, score_ref, out_ref, sems = blocks.rest[8:]
        tiles = sizes[0] // tile_pos
        parts = 2 if tile_pos % 32 == 0 else 1
        fine = tile_pos // parts

        def close(index):
            for n in range(parts):
                finish(sizes, fine, index * parts + n, state_refs, weight_ref, out_ref, partial_ref)
                tile_copy(sizes, fine, index * parts + n, out_ref, out_hbm, sems.at[index]).start()

        cases = blocks.cases() + [(jnp.logical_not(blocks.seen[0]), None, 0)]
        quick = (opened == tiles) & blocks.upper[0] & blocks.seen[0]

        @pl.when(quick)
        def _():
            for index in range(tiles):
                blocks.add(state_refs, index, blocks.key_bias, blocks.middle, blocks.reached)
            for index in range(tiles):
                close(index)

        few = blocks.reached <= fine

        @pl.when(few & blocks.seen[0])
        def _():
            biases = [(blocks.block_refs[0], blocks.key_bias[0], 0, sizes[0])]
            update(sizes, fine, 0, False, blocks.reached, blocks.query_ref, biases, state_refs)
            close(0)

        quick = quick | (few & blocks.seen[0])
        for wanted, biases, low in cases:

            def step(index, carry, biases=biases, low=low):
                if biases is not None:
                    blocks.add(state_refs, index, biases, low, blocks.reached)
                close(index)
                return carry

            lax.fori_loop(0, jnp.where(wanted & jnp.logical_not(quick), opened, 0), step, 0)

        score_of(partial_ref, score_ref)

        def wait(index, carry):
            for n in range(parts):
                tile_copy(sizes, fine, index * parts + n, out_ref, out_hbm, sems.at[index]).wait()
            return carry

        lax.fori_loop(0, opened, wait, 0)


def call(kernel, sizes, blocks, in_specs, out_specs, out_shape, scratch, aliases, operands):
    rows, heads, group, dim = sizes
    work = 4 * rows * heads * group * dim * rows * blocks
    return pl.pallas_call(
        kernel,
        out_shape=out_shape,
        in_specs=in_specs,
        out_specs=out_specs,
        scratch_shapes=scratch,
        input_output_aliases=aliases,
        cost_estimate=pl.CostEstimate(
            flops=work, bytes_accessed=rows * heads * group * dim * 8, transcendentals=work // (4 * dim)
        ),
        compiler_params=pltpu.CompilerParams(vmem_limit_bytes=32 * 1024 * 1024),
    )(*operands)


def attend_own(sizes, query, own):
    rows, heads, group, dim = sizes
    flat = (rows * heads * group, dim)
    tile_pos = math.gcd(rows, 128)
    return call(
        functools.partial(own_kernel, sizes, tile_pos),
        sizes,
        1,
        [HBM, VMEM],
        [VMEM] * 4,
        [jax.ShapeDtypeStruct(flat, jnp.bfloat16)] + [jax.ShapeDtypeStruct(flat, jnp.float32)] * 3,
        [pltpu.VMEM((rows, rows), jnp.float32), pltpu.SemaphoreType.DMA((rows // tile_pos,))],
        {},
        (pltpu.with_memory_space_constraint(query, pltpu.HBM), own),
    )


def attend_blocks(kernel, sizes, distances, query, own, choices, state, *more):
    rows, heads, group, dim = sizes
    flat = (rows * heads * group, dim)
    tile_pos = math.gcd(rows, 128)
    arrays, picks = [either for either, _ in choices], [pick for _, pick in choices]
    counts = [len(either) for either in arrays]
    operands = [query, own, *sum(arrays, []), *state, *more]
    in_specs = [VMEM] * len(operands)
    at = 2 + sum(counts)
    aliases = {at + n: n for n in range(3)}
    out_shape = [jax.ShapeDtypeStruct(flat, jnp.float32)] * 3
    out_specs = [VMEM] * 3
    scratch = []
    if more:
        again = len(more) > 1
        out_shape += [pltpu.HBM(flat, jnp.bfloat16), jax.ShapeDtypeStruct((rows, dim), jnp.float32)]
        out_shape += [jax.ShapeDtypeStruct((8, width), jnp.float32) for width in (LANES, rows)]
        out_specs += [HBM, VMEM, VMEM, VMEM]
        if again:
            in_specs[at + 4] = HBM
            aliases |= {at + 4 + n: 3 + n for n in range(4)}
        scratch += [pltpu.VMEM(flat, jnp.bfloat16), pltpu.SemaphoreType.DMA((rows // tile_pos,))]
    scratch += [pltpu.VMEM(own.shape, own.dtype) for n in counts if n > 1]
    outs = call(
        functools.partial(kernel, sizes, tile_pos, distances, counts, picks),
        sizes,
        len(choices),
        in_specs,
        out_specs,
        out_shape,
        scratch,
        aliases,
        operands,
    )
    return outs[:3], outs[3:]


def local(groups, devices, queries, keys, values, segments, score_weight):
    rows, heads, group, dim = queries.shape
    reach = rows * devices // 2
    back = min(devices - 1, -(-(reach - 1) // rows))
    sizes = (rows, heads, group, dim)

    def send(array, pairs):
        return lax.ppermute(array, "ctx", [(s, t) for s, t in pairs if t < devices])

    def send_whole(array, pairs):
        pairs = [(s, t) for s, t in pairs if t < devices]
        return lax.ppermute(array, ("groups", "ctx"), whole_permutation(pairs, groups, devices))

    weight = score_weight.reshape(heads * group, dim)
    own = pack(keys, values, segments)
    swap = [(i, i ^ 1) for i in range(devices)]
    gap = devices // 2
    around = {i: (i + 1) % devices for i in range(devices)} | {gap: 0, devices - 1: gap + 1}
    near = ([send(own, around.items()), send(own, swap)], lambda place: jnp.where(place == gap + 1, 1, 0))
    far = [send(own, [(i, i + 2) for i in range(parity, devices, 2)]) for parity in range(2)]
    by_parity = lambda place: place % 2
    query, *state = attend_own(sizes, queries.reshape(rows * heads * group, dim), own)
    relayed, query = lax.optimization_barrier((near[0][0], query))
    for distance in range(1, back + 1, 2):
        step = [near, (far, by_parity)][: back + 1 - distance]
        if distance + 2 <= back:
            relayed = send_whole(relayed, [(i, i + 2) for i in range(0, devices, 2)])
            next_near = ([relayed, send(far[0], swap)], by_parity)
            if distance + 3 <= back:
                starts = range(distance + 1, devices, 2), range(1, devices, 2)
                ways = [[(i, i + 2) for i in start] for start in starts]
                far = [send(far[0], ways[0]), send_whole(far[1], ways[1])]
            state, _ = attend_blocks(add_kernel, sizes, (distance, distance + 1), query, own, step, state)
            near = next_near
    state, outs = attend_blocks(finish_kernel, sizes, (distance,), query, own, step[:1], state, weight)
    if len(step) == 1:
        distance, step = devices, step * 2
    _, outs = attend_blocks(redo_kernel, sizes, (distance + 1,), query, own, step[1:], state, weight, *outs)
    attended, _, _, score = outs
    score = score[0]
    score = score + lax.ppermute(score, "head", [(0, 1), (1, 0)])
    return attended.reshape(queries.shape), score


def solution(mesh):
    return jax.shard_map(
        functools.partial(local, mesh.shape["groups"], mesh.shape["ctx"]),
        mesh=mesh,
        in_specs=(
            P(("groups", "ctx"), "head", None, None),
            P(("groups", "ctx"), "head", None),
            P(("groups", "ctx"), "head", None),
            P(("groups", "ctx")),
            P("head", None, None),
        ),
        out_specs=(P(("groups", "ctx"), "head", None, None), P(("groups", "ctx"))),
        check_vma=False,
    )
```

```python
import functools
import math

import jax
import jax.numpy as jnp
from jax import lax
from jax.experimental import pallas as pl
from jax.experimental.pallas import tpu as pltpu
from jax.sharding import PartitionSpec as P

HIDDEN = -1e30
LABEL_ROWS = 16
LANES = 128
VMEM = pl.BlockSpec(memory_space=pltpu.VMEM)
HBM = pl.BlockSpec(memory_space=pltpu.HBM)


def whole_permutation(pairs, groups, devices):
    onward = dict(pairs)
    targets = set(onward.values())
    ends = {}
    for start in onward.keys() - targets:
        end = start
        while end in onward:
            end = onward[end]
        ends[end] = start
    idle = [i for i in range(devices) if i not in onward and i not in targets] if groups > 1 else []
    return [
        (g * devices + s, g * devices + t) for g in range(groups) for s, t in sorted({**onward, **ends}.items())
    ] + [(g * devices + i, (g + 1) % groups * devices + i) for g in range(groups) for i in idle]


def pack_kernel(key_hbm, value_hbm, seg_hbm, out_ref, key_ref, value_ref, seg_ref, sems):
    copies = [
        pltpu.make_async_copy(source, target, sems.at[n])
        for n, (source, target) in enumerate(((key_hbm, key_ref), (value_hbm, value_ref), (seg_hbm, seg_ref)))
    ]
    for copy in copies:
        copy.start()
    rows, heads, dim = key_ref.shape
    for n, ref in enumerate((key_ref, value_ref)):
        copies[n].wait()
        for h in range(heads):
            out_ref[n * rows : (n + 1) * rows, h * dim : (h + 1) * dim] = ref[:, h, :]
    copies[2].wait()
    labels = (seg_ref[...] + 1).astype(jnp.float32).astype(jnp.bfloat16)
    empty = jnp.zeros((out_ref.shape[0] - 2 * rows - labels.shape[0], labels.shape[1]), jnp.bfloat16)
    out_ref[2 * rows :, :] = jnp.concatenate([labels, empty], axis=0)


def pack(keys, values, segments):
    rows, heads, dim = keys.shape
    lanes = heads * dim
    lines = -(-rows // lanes)
    segments = jnp.pad(segments, (0, lines * lanes - rows), constant_values=-1).reshape(lines, lanes)
    return pl.pallas_call(
        pack_kernel,
        out_shape=jax.ShapeDtypeStruct((2 * rows + lines + -lines % LABEL_ROWS, lanes), keys.dtype),
        in_specs=[HBM] * 3,
        out_specs=VMEM,
        scratch_shapes=[
            pltpu.VMEM(keys.shape, keys.dtype),
            pltpu.VMEM(values.shape, values.dtype),
            pltpu.VMEM(segments.shape, segments.dtype),
            pltpu.SemaphoreType.DMA((3,)),
        ],
        compiler_params=pltpu.CompilerParams(vmem_limit_bytes=4 * 1024 * 1024),
    )(*(pltpu.with_memory_space_constraint(x, pltpu.HBM) for x in (keys, values, segments)))


def labels_of(ref, rows):
    lines = -(-rows // ref.shape[1])
    grid = ref[2 * rows :, :].astype(jnp.float32)
    return jnp.concatenate([grid[n : n + 1, :] for n in range(lines)], axis=1)[:, :rows]


def fill_bias(bias_ref, labels, own, causal):
    rows = bias_ref.shape[0]
    own_column = jnp.transpose(jnp.broadcast_to(own, (LANES, rows)))[:, :1]
    seen = labels == own_column
    if causal:
        key = lax.broadcasted_iota(jnp.int32, (rows, rows), 1)
        seen = seen & (key <= lax.broadcasted_iota(jnp.int32, (rows, rows), 0))
    bias_ref[...] = jnp.where(seen, 0.0, HIDDEN)


def update(sizes, tile_pos, index, fresh, reached, query_ref, blocks, state_refs):
    rows, heads, group, dim = sizes
    scale = math.log2(math.e) / math.sqrt(dim)
    tile, half = tile_pos * heads * group, tile_pos * group
    start = pl.multiple_of(index * tile, tile)
    query = query_ref[pl.ds(start, tile), :].astype(jnp.float32).reshape(tile_pos, heads, group, dim)
    biases = []
    for _, bias, low, high in blocks:
        if bias is None:
            biases.append(None)
        elif isinstance(bias, jax.Array):
            biases.append(jnp.broadcast_to(bias[:, low:high], (half, high - low)))
        else:
            lines = [bias[pl.ds(index * tile_pos + p, 1), :][:, low:high] for p in range(tile_pos)]
            biases.append(jnp.concatenate([jnp.broadcast_to(line, (group, high - low)) for line in lines], axis=0))
    if not fresh:
        old_states = [ref[pl.ds(start, tile), :].reshape(tile_pos, heads, group, dim) for ref in state_refs]
    if reached is not None:
        row = lax.broadcasted_iota(jnp.int32, (half, dim), 0)
        changed = row < (reached - index * tile_pos) * group
    outs = [], [], []
    for h in range(heads):
        at = slice(h * dim, (h + 1) * dim)
        query_h = query[:, h].reshape(half, dim).astype(jnp.bfloat16)
        scores = []
        for (block_ref, _, low, high), bias in zip(blocks, biases):
            score = lax.dot_general(
                query_h, block_ref[low:high, at], (((1,), (1,)), ((), ())), preferred_element_type=jnp.float32
            )
            if bias is not None:
                score = score + bias
            scores.append([score[:, c : c + LANES] for c in range(0, high - low, LANES)])
        old = [] if fresh else [state[:, h].reshape(half, dim) for state in old_states]
        top = jnp.max(functools.reduce(jnp.maximum, sum(scores, old[:1])), axis=1, keepdims=True)
        weights = [[jnp.exp2((part - top) * scale) for part in parts] for parts in scores]
        total = functools.reduce(jnp.add, sum(weights, []))
        acc = None
        for (block_ref, _, low, high), parts in zip(blocks, weights):
            rounded = jnp.concatenate([part.astype(jnp.bfloat16) for part in parts], axis=1)
            part = jnp.dot(rounded, block_ref[rows + low : rows + high, at], preferred_element_type=jnp.float32)
            acc = part if acc is None else acc + part
        if not fresh:
            factor = jnp.exp2((old[0] - top) * scale)
            total = total + old[1] * factor
            acc = acc + old[2] * factor
        new = [jnp.broadcast_to(top, acc.shape), total, acc]
        if reached is not None:
            new = [jnp.where(changed, part, kept) for part, kept in zip(new, old)]
        for out, part in zip(outs, new):
            out.append(part.reshape(tile_pos, 1, group, dim))
    for ref, parts in zip(state_refs, outs):
        ref[pl.ds(start, tile), :] = jnp.concatenate(parts, axis=1).reshape(tile, dim)


def own_kernel(sizes, tile_pos, query_hbm, block_ref, query_ref, *refs):
    *state_refs, bias_ref, sems = refs
    rows, heads, group, _ = sizes
    tile = tile_pos * heads * group
    copies = [
        pltpu.make_async_copy(
            query_hbm.at[pl.ds(n * tile, tile), :], query_ref.at[pl.ds(n * tile, tile), :], sems.at[n]
        )
        for n in range(rows // tile_pos)
    ]
    for copy in copies:
        copy.start()
    own = labels_of(block_ref, rows)
    fill_bias(bias_ref, own, own, True)
    for n, copy in enumerate(copies):
        copy.wait()
        high = min(rows, -(-((n + 1) * tile_pos) // LANES) * LANES)
        update(sizes, tile_pos, n, True, None, query_ref, [(block_ref, bias_ref, 0, high)], state_refs)


class Blocks:
    def __init__(self, sizes, tile_pos, distances, counts, picks, refs):
        self.sizes, self.tile_pos = sizes, tile_pos
        rows = sizes[0]
        refs = list(refs)
        self.query_ref, own_ref = refs.pop(0), refs.pop(0)
        either_refs = [[refs.pop(0) for _ in range(n)] for n in counts]
        del refs[:3]
        copies = [refs.pop() for n in counts if n > 1]
        self.rest = refs
        place = lax.axis_index("ctx")
        self.block_refs = []
        for either, pick in zip(either_refs, picks):
            self.block_refs.append(either[0] if len(either) == 1 else copies.pop())
            if len(either) > 1:
                for n, ref in enumerate(either):

                    @pl.when(pick(place) == n)
                    def _(ref=ref, block_ref=self.block_refs[-1]):
                        block_ref[...] = ref[...]

        own = labels_of(own_ref, rows)
        first_label = jnp.min(own)
        self.reached = jnp.sum(jnp.where(own == first_label, 1.0, 0.0)).astype(jnp.int32)
        self.tiles_reached = (self.reached + tile_pos - 1) // tile_pos
        labels = [labels_of(ref, rows) for ref in self.block_refs]
        self.seen = [(jnp.max(label) == first_label) & (place >= far) for label, far in zip(labels, distances)]
        self.full = [see & (jnp.min(label) == first_label) for label, see in zip(labels, self.seen)]
        self.middle = rows // 2 // LANES * LANES
        self.upper = [
            jnp.max(label[:, : self.middle]) < first_label if self.middle else jnp.bool_(False) for label in labels
        ]
        self.key_bias = [jnp.where(label == first_label, 0.0, HIDDEN) for label in labels]

    def add(self, state_refs, index, biases, low=0, reached=None):
        blocks = [(self.block_refs[n], bias, low, self.sizes[0]) for n, bias in enumerate(biases)]
        update(self.sizes, self.tile_pos, index, False, reached, self.query_ref, blocks, state_refs)

    def cases(self):
        many = len(self.seen)
        cases = []
        for count in range(many, 0, -1):
            wanted = self.seen[count - 1]
            if count < many:
                wanted = wanted & jnp.logical_not(self.seen[count])
            nearer, bias = [None] * (count - 1), self.key_bias[count - 1]
            full, upper = self.full[count - 1], self.upper[count - 1]
            if count < many:
                cases.append((wanted, [*nearer, bias], 0))
                continue
            cases.append((wanted & full, [*nearer, None], 0))
            if many == 1 and self.middle:
                cases.append((wanted & upper, [bias], self.middle))
                wanted = wanted & jnp.logical_not(upper)
            cases.append((wanted & jnp.logical_not(full), [*nearer, bias], 0))
        return cases

    def add_all(self, state_refs):
        tiles = self.sizes[0] // self.tile_pos
        (wanted, biases, low), *others = self.cases()
        every = wanted & (self.reached == self.sizes[0])

        @pl.when(every)
        def _():
            for index in range(tiles):
                self.add(state_refs, index, biases, low)

        for wanted, biases, low in [(wanted & jnp.logical_not(every), biases, low), *others]:

            def step(index, carry, biases=biases, low=low):
                self.add(state_refs, index, biases, low, self.reached)
                return carry

            lax.fori_loop(0, jnp.where(wanted, self.tiles_reached, 0), step, 0)


def finish(sizes, tile_pos, index, state_refs, weight_ref, out_ref, partial_ref):
    rows, heads, group, dim = sizes
    per_pos = heads * group
    tile = tile_pos * per_pos
    start = pl.multiple_of(index * tile, tile)
    total = jnp.sum(state_refs[1][pl.ds(start, tile), :], axis=1, keepdims=True)
    attended = (state_refs[2][pl.ds(start, tile), :] * (1.0 / total)).astype(jnp.bfloat16)
    out_ref[pl.ds(start, tile), :] = attended
    weight = weight_ref[...].astype(jnp.float32)
    product = attended.astype(jnp.float32).reshape(tile_pos, per_pos, dim) * weight
    partial_ref[pl.ds(pl.multiple_of(index * tile_pos, tile_pos), tile_pos), :] = jnp.sum(product, axis=1)


def tile_copy(sizes, tile_pos, index, out_ref, out_hbm, sem):
    tile = tile_pos * sizes[1] * sizes[2]
    at = pl.ds(pl.multiple_of(index * tile, tile), tile)
    return pltpu.make_async_copy(out_ref.at[at, :], out_hbm.at[at, :], sem)


def score_of(partial_ref, score_ref):
    score_ref[...] = lax.dot_general(
        jnp.ones((score_ref.shape[0], partial_ref.shape[1]), jnp.float32),
        partial_ref[...],
        (((1,), (1,)), ((), ())),
        preferred_element_type=jnp.float32,
        precision=lax.Precision.HIGHEST,
    )


def add_kernel(sizes, tile_pos, distances, counts, picks, *refs):
    blocks = Blocks(sizes, tile_pos, distances, counts, picks, refs)
    blocks.add_all(blocks.rest[:3])


def finish_kernel(sizes, tile_pos, distances, counts, picks, *refs):
    blocks = Blocks(sizes, tile_pos, distances, counts, picks, refs)
    weight_ref, *state_refs = blocks.rest[:4]
    out_hbm, partial_ref, open_ref, score_ref, out_ref, sems = blocks.rest[4:]
    opened = jnp.where(blocks.full[0] & (blocks.reached < sizes[0]), blocks.tiles_reached, 0)
    open_ref[...] = jnp.broadcast_to(opened.astype(jnp.float32), open_ref.shape)
    tiles = sizes[0] // tile_pos
    cases = blocks.cases()
    all_open = opened == tiles

    @pl.when(all_open)
    def _():
        for index in range(tiles):
            blocks.add(state_refs, index, cases[0][1], cases[0][2], blocks.reached)

    def step(count, carry):
        index = tiles - 1 - count
        for wanted, biases, low in cases:

            @pl.when(wanted & (index < blocks.tiles_reached))
            def _(biases=biases, low=low):
                blocks.add(state_refs, index, biases, low, blocks.reached)

        @pl.when(index >= opened)
        def _():
            finish(sizes, tile_pos, index, state_refs, weight_ref, out_ref, partial_ref)
            tile_copy(sizes, tile_pos, index, out_ref, out_hbm, sems.at[index]).start()

        return carry

    every = (blocks.reached == sizes[0]) & blocks.seen[0]
    for wanted, biases, low in cases:

        @pl.when(wanted & every)
        def _(biases=biases, low=low):
            for index in range(tiles):
                blocks.add(state_refs, index, biases, low)
                finish(sizes, tile_pos, index, state_refs, weight_ref, out_ref, partial_ref)
                tile_copy(sizes, tile_pos, index, out_ref, out_hbm, sems.at[index]).start()

    lax.fori_loop(0, jnp.where(all_open | every, 0, tiles), step, 0)

    @pl.when(opened == 0)
    def _():
        score_of(partial_ref, score_ref)

    for index in range(tiles):

        @pl.when(index >= opened)
        def _(index=index):
            tile_copy(sizes, tile_pos, index, out_ref, out_hbm, sems.at[index]).wait()


def redo_kernel(sizes, tile_pos, distances, counts, picks, *refs):
    at = 2 + sum(counts) + 3
    weight_ref, _, _, open_ref, _ = refs[at : at + 5]
    opened = jnp.max(open_ref[...]).astype(jnp.int32)

    @pl.when(opened > 0)
    def _():
        blocks = Blocks(sizes, tile_pos, distances, counts, picks, refs)
        state_refs = blocks.rest[5:8]
        out_hbm, partial_ref, _, score_ref, out_ref, sems = blocks.rest[8:]
        tiles = sizes[0] // tile_pos
        parts = 2 if tile_pos % 32 == 0 else 1
        fine = tile_pos // parts

        def close(index):
            for n in range(parts):
                finish(sizes, fine, index * parts + n, state_refs, weight_ref, out_ref, partial_ref)
                tile_copy(sizes, fine, index * parts + n, out_ref, out_hbm, sems.at[index]).start()

        cases = blocks.cases() + [(jnp.logical_not(blocks.seen[0]), None, 0)]
        quick = (opened == tiles) & blocks.upper[0] & blocks.seen[0]

        @pl.when(quick)
        def _():
            for index in range(tiles):
                blocks.add(state_refs, index, blocks.key_bias, blocks.middle, blocks.reached)
            for index in range(tiles):
                close(index)

        few = blocks.reached <= fine

        @pl.when(few & blocks.seen[0])
        def _():
            biases = [(blocks.block_refs[0], blocks.key_bias[0], 0, sizes[0])]
            update(sizes, fine, 0, False, blocks.reached, blocks.query_ref, biases, state_refs)
            close(0)

        quick = quick | (few & blocks.seen[0])
        for wanted, biases, low in cases:

            def step(index, carry, biases=biases, low=low):
                if biases is not None:
                    blocks.add(state_refs, index, biases, low, blocks.reached)
                close(index)
                return carry

            lax.fori_loop(0, jnp.where(wanted & jnp.logical_not(quick), opened, 0), step, 0)

        score_of(partial_ref, score_ref)

        def wait(index, carry):
            for n in range(parts):
                tile_copy(sizes, fine, index * parts + n, out_ref, out_hbm, sems.at[index]).wait()
            return carry

        lax.fori_loop(0, opened, wait, 0)


def call(kernel, sizes, blocks, in_specs, out_specs, out_shape, scratch, aliases, operands):
    rows, heads, group, dim = sizes
    work = 4 * rows * heads * group * dim * rows * blocks
    return pl.pallas_call(
        kernel,
        out_shape=out_shape,
        in_specs=in_specs,
        out_specs=out_specs,
        scratch_shapes=scratch,
        input_output_aliases=aliases,
        cost_estimate=pl.CostEstimate(
            flops=work, bytes_accessed=rows * heads * group * dim * 8, transcendentals=work // (4 * dim)
        ),
        compiler_params=pltpu.CompilerParams(vmem_limit_bytes=32 * 1024 * 1024),
    )(*operands)


def attend_own(sizes, query, own):
    rows, heads, group, dim = sizes
    flat = (rows * heads * group, dim)
    tile_pos = math.gcd(rows, 128)
    return call(
        functools.partial(own_kernel, sizes, tile_pos),
        sizes,
        1,
        [HBM, VMEM],
        [VMEM] * 4,
        [jax.ShapeDtypeStruct(flat, jnp.bfloat16)] + [jax.ShapeDtypeStruct(flat, jnp.float32)] * 3,
        [pltpu.VMEM((rows, rows), jnp.float32), pltpu.SemaphoreType.DMA((rows // tile_pos,))],
        {},
        (pltpu.with_memory_space_constraint(query, pltpu.HBM), own),
    )


def attend_blocks(kernel, sizes, distances, query, own, choices, state, *more):
    rows, heads, group, dim = sizes
    flat = (rows * heads * group, dim)
    tile_pos = math.gcd(rows, 128)
    arrays, picks = [either for either, _ in choices], [pick for _, pick in choices]
    counts = [len(either) for either in arrays]
    operands = [query, own, *sum(arrays, []), *state, *more]
    in_specs = [VMEM] * len(operands)
    at = 2 + sum(counts)
    aliases = {at + n: n for n in range(3)}
    out_shape = [jax.ShapeDtypeStruct(flat, jnp.float32)] * 3
    out_specs = [VMEM] * 3
    scratch = []
    if more:
        again = len(more) > 1
        out_shape += [pltpu.HBM(flat, jnp.bfloat16), jax.ShapeDtypeStruct((rows, dim), jnp.float32)]
        out_shape += [jax.ShapeDtypeStruct((8, width), jnp.float32) for width in (LANES, rows)]
        out_specs += [HBM, VMEM, VMEM, VMEM]
        if again:
            in_specs[at + 4] = HBM
            aliases |= {at + 4 + n: 3 + n for n in range(4)}
        scratch += [pltpu.VMEM(flat, jnp.bfloat16), pltpu.SemaphoreType.DMA((rows // tile_pos,))]
    scratch += [pltpu.VMEM(own.shape, own.dtype) for n in counts if n > 1]
    outs = call(
        functools.partial(kernel, sizes, tile_pos, distances, counts, picks),
        sizes,
        len(choices),
        in_specs,
        out_specs,
        out_shape,
        scratch,
        aliases,
        operands,
    )
    return outs[:3], outs[3:]


def local(groups, devices, queries, keys, values, segments, score_weight):
    rows, heads, group, dim = queries.shape
    reach = rows * devices // 2
    back = min(devices - 1, -(-(reach - 1) // rows))
    sizes = (rows, heads, group, dim)

    def send(array, pairs):
        return lax.ppermute(array, "ctx", [(s, t) for s, t in pairs if t < devices])

    def send_whole(array, pairs):
        pairs = [(s, t) for s, t in pairs if t < devices]
        return lax.ppermute(array, ("groups", "ctx"), whole_permutation(pairs, groups, devices))

    weight = score_weight.reshape(heads * group, dim)
    own = pack(keys, values, segments)
    swap = [(i, i ^ 1) for i in range(devices)]
    near = ([send(own, [(i, (i + 1) % devices) for i in range(devices)])], None)
    far = [send(own, [(i, i + 2) for i in range(0, devices, 2)])]
    by_parity = lambda place: place % 2
    query, *state = attend_own(sizes, queries.reshape(rows * heads * group, dim), own)
    late, query = lax.optimization_barrier((own, query))
    far.append(send(late, [(i, i + 2) for i in range(1, devices, 2)]))
    relayed = near[0][0]
    for distance in range(1, back + 1, 2):
        step = [near, (far, by_parity)][: back + 1 - distance]
        if distance + 2 <= back:
            relayed = send_whole(relayed, [(i, i + 2) for i in range(0, devices, 2)])
            next_near = ([relayed, send(far[0], swap)], by_parity)
            if distance + 3 <= back:
                starts = range(distance + 1, devices, 2), range(1, devices, 2)
                ways = [[(i, i + 2) for i in start] for start in starts]
                far = [send(far[0], ways[0]), send_whole(far[1], ways[1])]
            state, _ = attend_blocks(add_kernel, sizes, (distance, distance + 1), query, own, step, state)
            near = next_near
    state, outs = attend_blocks(finish_kernel, sizes, (distance,), query, own, step[:1], state, weight)
    if len(step) == 1:
        distance, step = devices, step * 2
    _, outs = attend_blocks(redo_kernel, sizes, (distance + 1,), query, own, step[1:], state, weight, *outs)
    attended, _, _, score = outs
    score = score[0]
    score = score + lax.ppermute(score, "head", [(0, 1), (1, 0)])
    return attended.reshape(queries.shape), score


def solution(mesh):
    return jax.shard_map(
        functools.partial(local, mesh.shape["groups"], mesh.shape["ctx"]),
        mesh=mesh,
        in_specs=(
            P(("groups", "ctx"), "head", None, None),
            P(("groups", "ctx"), "head", None),
            P(("groups", "ctx"), "head", None),
            P(("groups", "ctx")),
            P("head", None, None),
        ),
        out_specs=(P(("groups", "ctx"), "head", None, None), P(("groups", "ctx"))),
        check_vma=False,
    )
```
